32 devices in a mesh: dp: 4 (over x, core), seq: 8 (over z, y).
Axes of the slice: x: 2, y: 2, z: 4, core: 2. Of those that a mesh axis runs over, the one named last changes fastest.
Arguments:
- q_lin: bfloat16 [4096, 256], P(('dp', 'seq')), parts along dimension 0, may hold values from -9 to 9
- k_lin: bfloat16 [4096, 256], P(('dp', 'seq')), parts along dimension 0, may hold values from -9 to 9
- q_win: bfloat16 [4096, 1024], P(('dp', 'seq')), parts along dimension 0, may hold values from -6 to 6
- k_win: bfloat16 [4096, 1024], P(('dp', 'seq')), parts along dimension 0, may hold values from -6 to 6
- values: bfloat16 [4096, 1024], P(('dp', 'seq')), parts along dimension 0, may hold values from -8 to 8
- grad_out: bfloat16 [4096, 1024], P(('dp', 'seq')), parts along dimension 0, may hold values from -8 to 8
Outputs:
- mixed: bfloat16 [4096, 1024], P(('dp', 'seq')), parts along dimension 0
- grad_q_lin: bfloat16 [4096, 256], P(('dp', 'seq')), parts along dimension 0
- grad_k_lin: bfloat16 [4096, 256], P(('dp', 'seq')), parts along dimension 0
- grad_q_win: bfloat16 [4096, 1024], P(('dp', 'seq')), parts along dimension 0
- grad_k_win: bfloat16 [4096, 1024], P(('dp', 'seq')), parts along dimension 0
- grad_values: bfloat16 [4096, 1024], P(('dp', 'seq')), parts along dimension 0
The draws below stay inside these ranges and needn't reach their ends.
There are 4 independent parts, one for each index of `dp`. The reference program is written for one: setup_inputs(seed, part) draws one part's arguments, and reference() takes and returns one part's arrays. A program takes and returns all parts, laid end to end along the dimension named above; each array names one. Nothing has to cross between parts.
All inputs are finite; a program needn't handle non-finite values.
Results may differ from the reference program's by a relative error of at most 0.0091.
Values may be sent and summed in bfloat16 or wider, within the bound.
A program may use at most 192 MiB of HBM per device.

```python
import math
import jax
import jax.numpy as jnp
from jax import lax

H = 16
DH = 64
FD = 16
WINDOW = 128
TOK_DEV = 128
SEQ_LEN = 1024


def window_jitter(key):
    row_width = H * DH
    jitter = jnp.clip(jax.random.normal(key, (SEQ_LEN, row_width)), -6.0, 6.0)
    return jitter


def draw_q_win(key, part):
    jitter = window_jitter(jax.random.fold_in(key, 11))
    result = jitter
    return result.astype(jnp.bfloat16)


def draw_k_win(key, part):
    jitter = window_jitter(jax.random.fold_in(key, 13))
    result = jitter
    return result.astype(jnp.bfloat16)


def shifted_field(key):
    row_width = H * DH
    segment = max(TOK_DEV // 4, 1)
    levels = jax.random.uniform(jax.random.fold_in(key, 3), (SEQ_LEN // segment + 1, row_width), minval=-2.0, maxval=2.0)
    level_rows = jnp.repeat(levels, segment, axis=0)[:SEQ_LEN]
    jitter = jnp.clip(jax.random.normal(jax.random.fold_in(key, 6), (SEQ_LEN, row_width)), -5.0, 5.0)
    return level_rows + jitter


def draw_values(key, part):
    return shifted_field(jax.random.fold_in(key, 21)).astype(jnp.bfloat16)


def draw_grad_out(key, part):
    return shifted_field(jax.random.fold_in(key, 22)).astype(jnp.bfloat16)


def shard_levels(stream_key, extent, pieces, low, top_value):
    def one(dim, shards_of):
        draws = jax.random.uniform(jax.random.fold_in(jax.random.fold_in(stream_key, 6), dim), (shards_of,), jnp.float32, low / len(pieces), top_value / len(pieces))
        return jnp.repeat(jnp.exp(draws), extent[dim] // shards_of).reshape((-1,) + (1,) * (len(extent) - dim - 1))

    factor_of = one(*pieces[0])
    for cut in pieces[1:]:
        factor_of = factor_of * one(*cut)
    return factor_of


def gaussian(own_key, shape, scale, limit, pieces=(), kind=jnp.bfloat16):
    values = scale * jax.random.normal(own_key, shape, jnp.float32)
    if pieces:
        values = values * shard_levels(own_key, shape, pieces, -0.22, 0.18)
    return jnp.clip(values, -limit, limit).astype(kind)


def setup_inputs(seed: int = 0, part: int = 0) -> dict:
    streams_of = jax.random.split(jax.random.key(seed), 7)
    own_keys = jax.random.split(jax.random.fold_in(streams_of[6], part), 7)
    return {
        "q_lin": gaussian(own_keys[0], (SEQ_LEN, H * FD), 1.5, 9.0, ((0, 8),)),
        "k_lin": gaussian(own_keys[1], (SEQ_LEN, H * FD), 1.5, 9.0, ((0, 8),)),
        "q_win": draw_q_win(jax.random.fold_in(jax.random.fold_in(streams_of[6], part), 71), part),
        "k_win": draw_k_win(jax.random.fold_in(jax.random.fold_in(streams_of[6], part), 71), part),
        "values": draw_values(jax.random.fold_in(jax.random.fold_in(streams_of[6], part), 71), part),
        "grad_out": draw_grad_out(jax.random.fold_in(jax.random.fold_in(streams_of[6], part), 71), part),
    }


HIGH = lax.Precision.HIGHEST

def feat_full(inputs):
    feat_depth = inputs.shape[-1]
    leading = inputs.shape[:-1]
    ones_col = jnp.ones(leading + (1,), inputs.dtype)
    square = (inputs[..., :, None] * inputs[..., None, :]).reshape(leading + (feat_depth * feat_depth,))
    linear_factor = 1.0 / math.sqrt(math.sqrt(feat_depth))
    return jnp.concatenate([ones_col, inputs * linear_factor, square / math.sqrt(2.0 * feat_depth)], -1)

def linear_pieces(lin_query, lin_key):
    inv_root = 1.0 / math.sqrt(lin_query.shape[-1])
    scores = jnp.einsum('thf,shf->hts', lin_query, lin_key, precision=HIGH) * inv_root
    tok_count = lin_query.shape[0]
    causal = jnp.arange(tok_count, dtype=jnp.int32)[:, None] >= jnp.arange(tok_count, dtype=jnp.int32)[None, :]
    kernel = jnp.where(causal[None], 1.0 + scores + 0.5 * scores * scores, 0.0)
    return (scores, kernel, causal)

def linear_grads(lin_query, lin_key, value_f32, d_numer, d_denom, prev_state, prev_norm, next_state, next_norm, scores, kernel, causal, key_feat, query_pull, key_pull):
    inv_root = 1.0 / math.sqrt(lin_query.shape[-1])
    d_kernel = jnp.einsum('thd,shd->hts', d_numer, value_f32, precision=HIGH) + d_denom.T[:, :, None]
    d_scores = jnp.where(causal[None], d_kernel, 0.0) * (1.0 + scores)
    d_values = jnp.einsum('hts,thd->shd', kernel, d_numer, precision=HIGH) + jnp.einsum('shf,hfd->shd', key_feat, next_state, precision=HIGH)
    d_qfeat = jnp.einsum('hfd,thd->thf', prev_state, d_numer, precision=HIGH) + prev_norm[None] * d_denom[:, :, None]
    d_kfeat = jnp.einsum('hfd,shd->shf', next_state, value_f32, precision=HIGH) + next_norm[None]
    d_query = jnp.einsum('hts,shf->thf', d_scores, lin_key, precision=HIGH) * inv_root + query_pull(d_qfeat)[0]
    d_key = jnp.einsum('hts,thf->shf', d_scores, lin_query, precision=HIGH) * inv_root + key_pull(d_kfeat)[0]
    return (d_query, d_key, d_values)

def window_block(query, key_rows, value_rows, grads, start):
    query = query.astype(jnp.float32)
    key_rows = key_rows.astype(jnp.float32)
    value_rows = value_rows.astype(jnp.float32)
    grads = grads.astype(jnp.float32)
    q_count = query.shape[0]
    k_count = key_rows.shape[0]
    inv_root = 1.0 / math.sqrt(query.shape[2])
    query_pos = start + jnp.arange(q_count, dtype=jnp.int32)[:, None]
    key_pos = start - (k_count - q_count) + jnp.arange(k_count, dtype=jnp.int32)[None, :]
    allowed = (key_pos <= query_pos) & (key_pos > query_pos - WINDOW) & (key_pos >= 0)
    logits = jnp.einsum('thd,shd->hts', query, key_rows, precision=HIGH) * inv_root
    logits = jnp.where(allowed[None], logits, -1e+30)
    shifted = jnp.exp(logits - lax.optimization_barrier(jnp.max(logits, -1, keepdims=True)))
    attn_weights = shifted / lax.optimization_barrier(jnp.sum(shifted, -1, keepdims=True))
    attn_low = lax.optimization_barrier(attn_weights.astype(jnp.bfloat16)).astype(jnp.float32)
    result = jnp.einsum('hts,shd->thd', attn_low, value_rows, precision=HIGH)
    d_attn = jnp.einsum('thd,shd->hts', grads, value_rows, precision=HIGH)
    d_values = jnp.einsum('hts,thd->shd', attn_low, grads, precision=HIGH)
    row_inner = lax.optimization_barrier(jnp.sum(grads * result, -1)).T
    d_logits = attn_weights * (d_attn - row_inner[:, :, None])
    d_logits = lax.optimization_barrier(d_logits.astype(jnp.bfloat16)).astype(jnp.float32)
    d_query = jnp.einsum('hts,shd->thd', d_logits, key_rows, precision=HIGH) * inv_root
    d_keys = jnp.einsum('hts,thd->shd', d_logits, query, precision=HIGH) * inv_root
    return (result, d_query, d_keys, d_values)

def reference(q_lin, k_lin, q_win, k_win, values, grad_out):
    total = q_lin.shape[0]
    blocks = total // TOK_DEV
    row_width = H * DH
    pad_keys = jnp.concatenate([jnp.zeros((WINDOW, row_width), k_win.dtype), k_win], 0)
    pad_values = jnp.concatenate([jnp.zeros((WINDOW, row_width), values.dtype), values], 0)

    def window_one(block_index):
        low_row = (block_index * TOK_DEV).astype(jnp.int32)
        return window_block(lax.dynamic_slice_in_dim(q_win, low_row, TOK_DEV, 0).reshape(TOK_DEV, H, DH), lax.dynamic_slice_in_dim(pad_keys, low_row, TOK_DEV + WINDOW, 0).reshape(TOK_DEV + WINDOW, H, DH), lax.dynamic_slice_in_dim(pad_values, low_row, TOK_DEV + WINDOW, 0).reshape(TOK_DEV + WINDOW, H, DH), lax.dynamic_slice_in_dim(grad_out, low_row, TOK_DEV, 0).reshape(TOK_DEV, H, DH), low_row)
    win_out, win_dq, win_dk, win_dv = lax.map(window_one, jnp.arange(blocks, dtype=jnp.int32))

    def settle(grads_all):
        own_part = grads_all[:, WINDOW:]
        moved = jnp.concatenate([grads_all[1:, :WINDOW], jnp.zeros_like(grads_all[:1, :WINDOW])], 0)
        return own_part.at[:, TOK_DEV - WINDOW:].add(moved)

    def split(array, feat_depth):
        return array.reshape(blocks, TOK_DEV, H, feat_depth).astype(jnp.float32)
    block_q = split(q_lin, FD)
    block_k = split(k_lin, FD)
    block_v = split(values, DH)
    block_g = split(grad_out, DH)
    feats = 1 + FD + FD * FD
    empty = (jnp.zeros((H, feats, DH), jnp.float32), jnp.zeros((H, feats), jnp.float32))

    def forward_step(carry, inputs):
        run_state, run_norm = carry
        lin_query, lin_key, value_f32 = inputs
        scores, kernel, causal = linear_pieces(lin_query, lin_key)
        query_feat = feat_full(lin_query)
        key_feat = feat_full(lin_key)
        numer = jnp.einsum('thf,hfd->thd', query_feat, run_state, precision=HIGH) + jnp.einsum('hts,shd->thd', kernel, value_f32, precision=HIGH)
        denom = jnp.einsum('thf,hf->th', query_feat, run_norm, precision=HIGH) + lax.optimization_barrier(jnp.sum(kernel, -1)).T
        own_state = jnp.einsum('thf,thd->hfd', key_feat, value_f32, precision=HIGH)
        own_norm = lax.optimization_barrier(jnp.sum(key_feat, 0))
        return ((run_state + own_state, run_norm + own_norm), (numer / denom[:, :, None], denom, run_state, run_norm))
    _, (lin_out, denom, prev_state, prev_norm) = lax.scan(forward_step, empty, (block_q, block_k, block_v))
    d_numer = block_g / denom[..., None]
    d_denom = -lax.optimization_barrier(jnp.sum(block_g * lin_out, -1)) / denom

    def backward_step(carry, inputs):
        run_state, run_norm = carry
        lin_query, numer_grad, denom_grad = inputs
        query_feat = feat_full(lin_query)
        own_state = jnp.einsum('thf,thd->hfd', query_feat, numer_grad, precision=HIGH)
        own_norm = jnp.einsum('thf,th->hf', query_feat, denom_grad, precision=HIGH)
        return ((run_state + own_state, run_norm + own_norm), (run_state, run_norm))
    _, (next_state, next_norm) = lax.scan(backward_step, empty, (block_q, d_numer, d_denom), reverse=True)

    def grad_one(inputs):
        lin_query, lin_key, value_f32, numer_grad, denom_grad, state_before, norm_before, state_after, norm_after = inputs
        scores, kernel, causal = linear_pieces(lin_query, lin_key)
        key_feat, key_pull = jax.vjp(feat_full, lin_key)
        query_feat, query_pull = jax.vjp(feat_full, lin_query)
        return linear_grads(lin_query, lin_key, value_f32, numer_grad, denom_grad, state_before, norm_before, state_after, norm_after, scores, kernel, causal, key_feat, query_pull, key_pull)
    lin_dq, lin_dk, lin_dv = lax.map(grad_one, (block_q, block_k, block_v, d_numer, d_denom, prev_state, prev_norm, next_state, next_norm))
    mixed = (lin_out.reshape(total, row_width) + win_out.reshape(total, row_width)).astype(jnp.bfloat16)
    grad_q_lin = lin_dq.reshape(total, H * FD).astype(jnp.bfloat16)
    grad_k_lin = lin_dk.reshape(total, H * FD).astype(jnp.bfloat16)
    grad_q_win = win_dq.reshape(total, row_width).astype(jnp.bfloat16)
    grad_k_win = settle(win_dk).reshape(total, row_width).astype(jnp.bfloat16)
    grad_values = (lin_dv.reshape(total, row_width) + settle(win_dv).reshape(total, row_width)).astype(jnp.bfloat16)
    return (mixed, grad_q_lin, grad_k_lin, grad_q_win, grad_k_win, grad_values)
```

```python
import functools

import jax
import jax.numpy as jnp
from jax import lax
from jax.experimental import pallas as pl
from jax.experimental.pallas import tpu as pltpu
from jax.sharding import PartitionSpec as P

FD = 16
DH = 64
NF = 160
F32 = jnp.float32
BF = jnp.bfloat16


def dot(a, b, ca, cb):
    return lax.dot_general(a, b, (((ca,), (cb,)), ((), ())), preferred_element_type=F32)


def turned(x, d):
    return x if d == 0 else jnp.concatenate([x[d:], x[:d]], 0)


def features(x, query):
    pair = 1.0 / 16.0 if query else 1.0
    parts = [x * x * (pair * 0.5 if query else 1.0)]
    scaled = x * pair
    for d in range(1, 8):
        parts.append(scaled * turned(x, d))
    parts.append(scaled[:8] * x[8:])
    parts.append(x * 0.25 if query else x)
    row = lax.broadcasted_iota(jnp.int32, (8, x.shape[1]), 0)
    parts.append(jnp.where(row == 0, 1.0, 0.0).astype(F32))
    return jnp.concatenate(parts, 0)


def pull(x, d_feat, query):
    pair = 1.0 / 16.0 if query else 1.0
    total = d_feat[0:16] * x * (pair if query else 2.0)
    cross = jnp.zeros_like(x)
    for d in range(1, 8):
        part = d_feat[16 * d : 16 * d + 16]
        cross = cross + part * turned(x, d) + turned(part * x, 16 - d)
    last = d_feat[128:136]
    cross = cross + jnp.concatenate([last * x[8:], last * x[:8]], 0)
    line = d_feat[136:152]
    return total + cross * pair + line * (0.25 if query else 1.0)


def kernel(n, axis, ql, kl, qw, kw, v, g, mixed, gql, gkl, gqw, gkw, gv,
           qt, kt, qf, kf, kern, nown, nall, ncol, s_own, f_in, f_out,
           sb_own, b_in, b_out, rden, dn, win, dwk, dwv, dden, stat_t, stat_in,
           nbown, nball, nbcol, kprev, vprev, qnext, gnext, dqt, dkt,
           halo_s, halo_r, n_s, n_r, nb_s, nb_r, f_s, f_r, b_s, b_r, st_s, st_r):
    me = lax.axis_index(axis)
    tok = ql.shape[0]
    pairs = v.shape[1] // 128
    heads = 2 * pairs
    first, last = me == 0, me == n - 1
    lane = lax.broadcasted_iota(jnp.int32, (1, 128), 1)
    half = [(lane < DH).astype(F32).astype(BF), (lane >= DH).astype(F32).astype(BF)]
    rows = lax.broadcasted_iota(jnp.int32, (tok, tok), 0)
    cols = lax.broadcasted_iota(jnp.int32, (tok, tok), 1)
    lanes2 = lax.broadcasted_iota(jnp.int32, (tok, 128), 1)
    causal = cols <= rows

    def cut(p):
        return pl.ds(pl.multiple_of(p * 128, 128), 128)

    def frow(h):
        return pl.ds(pl.multiple_of(h * FD, FD), FD)

    def remote(src, dst, ss, rs, to):
        return pltpu.make_async_remote_copy(
            src_ref=src, dst_ref=dst, send_sem=ss, recv_sem=rs,
            device_id={axis: to}, device_id_type=pl.DeviceIdType.MESH)

    def halo(which, p):
        src = (kw, v, qw, g)[which]
        dst = (kprev, vprev, qnext, gnext)[which]
        to = me + 1 if which < 2 else me - 1
        return remote(src.at[:, cut(p)], dst.at[:, cut(p)],
                      halo_s.at[which, p], halo_r.at[which, p], to)

    def f_copy(p):
        return remote(f_out.at[p], f_in.at[p], f_s.at[p], f_r.at[p], me + 1)

    def b_copy(p):
        return remote(b_out.at[p], b_in.at[p], b_s.at[p], b_r.at[p], me - 1)

    def n_copy(to):
        return remote(nown, nall.at[me], n_s.at[to], n_r.at[me], to)

    def nb_copy(to):
        return remote(nbown, nball.at[me], nb_s.at[to], nb_r.at[me], to)

    def n_from(j):
        return remote(nown, nall.at[j], n_s.at[j], n_r.at[j], j)

    def nb_from(j):
        return remote(nbown, nball.at[j], nb_s.at[j], nb_r.at[j], j)

    def stats_copy():
        return remote(stat_t, stat_in, st_s, st_r, me - 1)

    def loop(low, high, body):
        def one(i, c):
            body(i)
            return c
        lax.fori_loop(low, high, one, 0)

    barrier = pltpu.get_barrier_semaphore()
    for d in range(1, n):
        pl.semaphore_signal(barrier, inc=1, device_id={axis: lax.rem(me + d, n)},
                            device_id_type=pl.DeviceIdType.MESH)

    qt[...] = ql[...].astype(F32).T
    kt[...] = kl[...].astype(F32).T
    nown[...] = jnp.zeros_like(nown)
    nbown[...] = jnp.zeros_like(nbown)
    dden[...] = jnp.zeros_like(dden)
    ones8 = jnp.ones((8, tok), BF)

    def phase_a(p):
        got = []
        for hh in range(2):
            h = 2 * p + hh
            kfeat = features(kt[frow(h), :], False).astype(BF)
            kf[h] = kfeat
            qf[h] = features(qt[frow(h), :], True).astype(BF)
            nown[pl.ds(h, 1), 0:NF] = dot(ones8, kfeat, 1, 1)[0:1]
            got.append(dot(kfeat, v[:, cut(p)], 1, 0))
        s_own[p] = jnp.where(lane < DH, got[0], got[1])

    loop(0, pairs, phase_a)
    pl.semaphore_wait(barrier, n - 1)
    loop(me + 1, n, lambda j: n_copy(j).start())

    def send_halo(p):
        @pl.when(jnp.logical_not(last))
        def _():
            halo(0, p).start()
            halo(1, p).start()

        @pl.when(jnp.logical_not(first))
        def _():
            halo(2, p).start()
            halo(3, p).start()

    @pl.when(first)
    def _():
        kprev[...] = jnp.zeros_like(kprev)
        vprev[...] = jnp.zeros_like(vprev)
        f_in[...] = jnp.zeros_like(f_in)

    @pl.when(last)
    def _():
        qnext[...] = jnp.zeros_like(qnext)
        gnext[...] = jnp.zeros_like(gnext)
        stat_in[...] = jnp.zeros_like(stat_in)
        b_in[...] = jnp.zeros_like(b_in)

    def gathered(low, high, arrive, slots):
        def one(j, total):
            arrive(j).wait_recv()
            return total + slots[j]
        total = lax.fori_loop(low, high, one, jnp.zeros(nown.shape, F32))
        full = jnp.concatenate([total, jnp.zeros((128 - heads, nown.shape[1]), F32)], 0)
        return full.T[0:NF].astype(BF)

    loop(0, pairs, send_halo)
    ncol[...] = gathered(0, me, n_from, nall)

    def lin_scores(h):
        return dot(qt[frow(h), :].astype(BF), kt[frow(h), :].astype(BF), 0, 0) * 0.25

    def phase_c(p):
        inv = []
        for hh in range(2):
            h = 2 * p + hh
            s = lin_scores(h)
            kk = jnp.where(causal, 1.0 + s + 0.5 * s * s, 0.0)
            kern[h] = kk.astype(BF)
            prior = dot(qf[h], ncol[...], 0, 0)
            den = jnp.sum(kk + jnp.where(lanes2 == h, prior, 0.0), 1, keepdims=True)
            inv.append(1.0 / den)
        r = jnp.where(lane < DH, inv[0], inv[1])
        rden[p] = r
        low = (g[:, cut(p)].astype(F32) * r).astype(BF)
        dn[:, cut(p)] = low
        sb_own[p] = jnp.where(lane < DH, dot(qf[2 * p], low, 1, 0), dot(qf[2 * p + 1], low, 1, 0))

    loop(0, pairs, phase_c)

    def window(p):
        @pl.when(jnp.logical_not(first))
        def _():
            halo(0, p).wait_recv()
            halo(1, p).wait_recv()
        c = cut(p)
        q, k, vv, gg, kp, vp = qw[:, c], kw[:, c], v[:, c], g[:, c], kprev[:, c], vprev[:, c]
        prior = jnp.logical_and(cols > rows, me > 0)
        keep = []
        for hh in range(2):
            h = 2 * p + hh
            qm, gm = q * half[hh], gg * half[hh]
            so = jnp.where(causal, dot(qm, k, 1, 1) * 0.125, -1e30)
            sp = jnp.where(prior, dot(qm, kp, 1, 1) * 0.125, -1e30)
            m = jnp.max(jnp.maximum(so, sp), 1, keepdims=True)
            eo, ep = jnp.exp(so - m), jnp.exp(sp - m)
            total = jnp.sum(eo + ep, 1, keepdims=True)
            inv = 1.0 / total
            ao, ap = eo * inv, ep * inv
            lo, lp = ao.astype(BF), ap.astype(BF)
            res = dot(lo, vv, 1, 0) + dot(lp, vp, 1, 0)
            inner = jnp.sum(gm.astype(F32) * res, 1, keepdims=True)
            do = (ao * (dot(gm, vv, 1, 1) - inner)).astype(BF)
            dp = (ap * (dot(gm, vp, 1, 1) - inner)).astype(BF)
            dq = dot(do, k, 1, 0) + dot(dp, kp, 1, 0)
            keep.append((res, dq, dot(do, q, 0, 0), dot(lo, gg, 0, 0)))
            logsum = m + jnp.log(total)
            dden[...] += jnp.where(lanes2 == h, logsum, 0.0) + jnp.where(lanes2 == heads + h, inner, 0.0)
        res, dq, dk, dv = [jnp.where(lane < DH, a, b) for a, b in zip(*keep)]
        win[:, c] = res
        gqw[:, c] = (dq * 0.125).astype(BF)
        dwk[:, c] = dk
        dwv[:, c] = dv

    def f_step(p):
        @pl.when(jnp.logical_not(first))
        def _():
            f_copy(p).wait_recv()

        @pl.when(jnp.logical_not(last))
        def _():
            f_out[p] = (f_in[p].astype(F32) + s_own[p]).astype(BF)
            f_copy(p).start()

    def b_step(p):
        @pl.when(jnp.logical_not(last))
        def _():
            b_copy(p).wait_recv()

        @pl.when(jnp.logical_not(first))
        def _():
            b_out[p] = (b_in[p].astype(F32) + sb_own[p]).astype(BF)
            b_copy(p).start()

    def wave(j):
        fp = j - me

        @pl.when(jnp.logical_and(fp >= 0, fp < pairs))
        def _():
            f_step(fp)
        bp = j - (n - 1 - me)

        @pl.when(jnp.logical_and(bp >= 0, bp < pairs))
        def _():
            b_step(bp)

        @pl.when(j < pairs)
        def _():
            window(j)

    loop(0, pairs + n - 1, wave)
    stat_t[...] = dden[...].T[0 : 2 * heads]
    dden[...] = jnp.zeros_like(dden)

    @pl.when(jnp.logical_not(first))
    def _():
        stats_copy().start()

    def phase_d(p):
        c = cut(p)
        vv, low, r, pre = v[:, c], dn[:, c], rden[p], f_in[p]
        num = [dot(kern[2 * p + hh], vv, 1, 0) + dot(qf[2 * p + hh], pre, 0, 0) for hh in range(2)]
        out = jnp.where(lane < DH, num[0], num[1]) * r
        mixed[:, c] = (out + win[:, c]).astype(BF)
        prod = g[:, c].astype(F32) * out * r
        both = jnp.concatenate([pre, ncol[...]], 1)
        for hh in range(2):
            h = 2 * p + hh
            dd = -jnp.sum(jnp.where((lane < DH) == (hh == 0), prod, 0.0), 1, keepdims=True)
            spread = jnp.where(lanes2 == h, dd, 0.0)
            dden[...] += spread
            dm = low * half[hh]
            ds = jnp.where(causal, dot(dm, vv, 1, 1) + dd, 0.0) * (1.0 + lin_scores(h))
            ds = ds.astype(BF)
            d_feat = dot(both, jnp.concatenate([dm, spread.astype(BF)], 1), 1, 1)
            x = qt[frow(h), :]
            dqt[frow(h), :] = dot(kt[frow(h), :].astype(BF), ds, 1, 1) * 0.25 + pull(x, d_feat, True)
            dkt[frow(h), :] = dot(x.astype(BF), ds, 1, 0) * 0.25

    loop(0, pairs, phase_d)
    gql[...] = dqt[...].T.astype(BF)
    dden[...] = dden[...].T

    def back_norm(h):
        one = jnp.broadcast_to(dden[pl.ds(h, 1), :], (8, tok)).astype(BF)
        nbown[pl.ds(h, 1), 0:NF] = dot(one, qf[h], 1, 1)[0:1]

    loop(0, heads, back_norm)
    loop(0, me, lambda j: nb_copy(j).start())

    @pl.when(jnp.logical_not(last))
    def _():
        stats_copy().wait_recv()

    def key_side(p):
        @pl.when(jnp.logical_not(last))
        def _():
            halo(2, p).wait_recv()
            halo(3, p).wait_recv()
        c = cut(p)
        k, vv, q, gg = kw[:, c], v[:, c], qnext[:, c], gnext[:, c]
        live = jnp.logical_and(rows > cols, me < n - 1)
        keep = []
        for hh in range(2):
            h = 2 * p + hh
            s = dot(k * half[hh], q, 1, 1) * 0.125
            a = jnp.exp(jnp.where(live, s - stat_in[pl.ds(h, 1), :], -1e30))
            ds = a * (dot(vv * half[hh], gg, 1, 1) - stat_in[pl.ds(heads + h, 1), :])
            keep.append((dot(ds.astype(BF), q, 1, 0), dot(a.astype(BF), gg, 1, 0)))
        dk, dv = [jnp.where(lane < DH, a, b) for a, b in zip(*keep)]
        gkw[:, c] = ((dwk[:, c] + dk) * 0.125).astype(BF)
        dwv[:, c] += dv

    loop(0, pairs, key_side)
    nbcol[...] = gathered(me + 1, n, nb_from, nball)

    def phase_e(p):
        c = cut(p)
        vv, low, post = v[:, c], dn[:, c], b_in[p]
        both = jnp.concatenate([post, nbcol[...]], 1)
        got = []
        for hh in range(2):
            h = 2 * p + hh
            got.append(dot(kern[h], low, 0, 0) + dot(kf[h], post, 0, 0))
            pick = jnp.where(lanes2 == h, 1.0, 0.0).astype(BF)
            d_feat = dot(both, jnp.concatenate([vv * half[hh], pick], 1), 1, 1)
            dkt[frow(h), :] += pull(kt[frow(h), :], d_feat, False)
        gv[:, c] = (jnp.where(lane < DH, got[0], got[1]) + dwv[:, c]).astype(BF)

    loop(0, pairs, phase_e)
    gkl[...] = dkt[...].T.astype(BF)

    def drain(p):
        @pl.when(jnp.logical_not(last))
        def _():
            halo(0, p).wait_send()
            halo(1, p).wait_send()
            f_copy(p).wait_send()

        @pl.when(jnp.logical_not(first))
        def _():
            halo(2, p).wait_send()
            halo(3, p).wait_send()
            b_copy(p).wait_send()

    loop(0, pairs, drain)
    loop(me + 1, n, lambda j: n_copy(j).wait_send())
    loop(0, me, lambda j: nb_copy(j).wait_send())

    @pl.when(jnp.logical_not(first))
    def _():
        stats_copy().wait_send()


def local(n, axis, *args):
    ql, v = args[0], args[4]
    tok, width = v.shape
    lin = ql.shape[1]
    pairs = width // 128
    heads = 2 * pairs
    vm = pltpu.VMEM
    dma = pltpu.SemaphoreType.DMA
    state16 = vm((pairs, NF, 128), BF)
    state32 = vm((pairs, NF, 128), F32)
    rows = vm((heads, 256), F32)
    wide32 = vm((tok, width), F32)
    wide16 = vm((tok, width), BF)
    lin32 = vm((lin, tok), F32)
    scratch = [
        lin32, lin32, vm((heads, NF, tok), BF), vm((heads, NF, tok), BF), vm((heads, tok, tok), BF),
        rows, vm((n, heads, 256), F32), vm((NF, 128), BF), state32, state16, state16,
        state32, state16, state16, vm((pairs, tok, 128), F32), wide16, wide32, wide32, wide32,
        vm((tok, 128), F32), vm((2 * heads, tok), F32), vm((2 * heads, tok), F32),
        rows, vm((n, heads, 256), F32), vm((NF, 128), BF),
        wide16, wide16, wide16, wide16, lin32, lin32,
        dma((4, pairs)), dma((4, pairs)), dma((n,)), dma((n,)), dma((n,)), dma((n,)),
        dma((pairs,)), dma((pairs,)), dma((pairs,)), dma((pairs,)), dma, dma,
    ]
    order = (v, ql, ql, v, v, v)
    whole = pl.BlockSpec(memory_space=pltpu.VMEM)
    return pl.pallas_call(
        functools.partial(kernel, n, axis),
        out_shape=tuple(jax.ShapeDtypeStruct(a.shape, BF) for a in order),
        in_specs=[whole] * 6,
        out_specs=tuple([whole] * 6),
        scratch_shapes=scratch,
        compiler_params=pltpu.CompilerParams(
            collective_id=0, has_side_effects=True, vmem_limit_bytes=40 * 1024 * 1024),
    )(*args)


def solution(mesh):
    place = P(("dp", "seq"), None)
    return jax.shard_map(
        functools.partial(local, mesh.shape["seq"], "seq"),
        mesh=mesh,
        in_specs=(place,) * 6,
        out_specs=(place,) * 6,
        check_vma=False,
    )
```

```python
import functools

import jax
import jax.numpy as jnp
from jax import lax
from jax.experimental import pallas as pl
from jax.experimental.pallas import tpu as pltpu
from jax.sharding import PartitionSpec as P

FD = 16
DH = 64
NF = 160
F32 = jnp.float32
BF = jnp.bfloat16


def dot(a, b, ca, cb):
    return lax.dot_general(a, b, (((ca,), (cb,)), ((), ())), preferred_element_type=F32)


def turned(x, d):
    return x if d == 0 else jnp.concatenate([x[d:], x[:d]], 0)


def features(x, query):
    pair = 1.0 / 16.0 if query else 1.0
    parts = [x * x * (pair * 0.5 if query else 1.0)]
    scaled = x * pair
    for d in range(1, 8):
        parts.append(scaled * turned(x, d))
    parts.append(scaled[:8] * x[8:])
    parts.append(x * 0.25 if query else x)
    row = lax.broadcasted_iota(jnp.int32, (8, x.shape[1]), 0)
    parts.append(jnp.where(row == 0, 1.0, 0.0).astype(F32))
    return jnp.concatenate(parts, 0)


def pull(x, d_feat, query):
    pair = 1.0 / 16.0 if query else 1.0
    total = d_feat[0:16] * x * (pair if query else 2.0)
    cross = jnp.zeros_like(x)
    for d in range(1, 8):
        part = d_feat[16 * d : 16 * d + 16]
        cross = cross + part * turned(x, d) + turned(part * x, 16 - d)
    last = d_feat[128:136]
    cross = cross + jnp.concatenate([last * x[8:], last * x[:8]], 0)
    line = d_feat[136:152]
    return total + cross * pair + line * (0.25 if query else 1.0)


def kernel(n, axis, ql_h, kl_h, qw_h, kw_h, v_h, g_h, mixed, gql, gkl, gqw, gkw, gv,
           ql, kl, qw, kw, v, g,
           qt, kt, qf, kf, kern, plus, ksum, nown, nall, ncol, s_own, f_in, f_out,
           sb_own, b_in, b_out, rden, dn, win, dwk, dwv, dden, stat, stat_t, stat_in,
           nbown, nball, nbcol, kprev, vprev, qnext, gnext, dqt, dkt,
           in_s, halo_s, halo_r, n_s, n_r, nb_s, nb_r, f_s, f_r, b_s, b_r, st_s, st_r):
    me = lax.axis_index(axis)
    tok = ql.shape[0]
    pairs = v.shape[1] // 128
    heads = 2 * pairs
    first, last = me == 0, me == n - 1
    lane = lax.broadcasted_iota(jnp.int32, (1, 128), 1)
    half = [(lane < DH).astype(F32).astype(BF), (lane >= DH).astype(F32).astype(BF)]
    rows = lax.broadcasted_iota(jnp.int32, (tok, tok), 0)
    cols = lax.broadcasted_iota(jnp.int32, (tok, tok), 1)
    lanes2 = lax.broadcasted_iota(jnp.int32, (tok, 128), 1)
    causal = cols <= rows
    causal2 = jnp.concatenate([causal, causal], 0)

    def cut(p):
        return pl.ds(pl.multiple_of(p * 128, 128), 128)

    def prow(p):
        return pl.ds(pl.multiple_of(p * 2 * FD, 2 * FD), 2 * FD)

    def both_halves(x):
        return jnp.concatenate([x * half[0], x * half[1]], 0)

    def pick(x):
        m = x.shape[0] // 2
        return jnp.where(lane < DH, x[:m], x[m:])

    def remote(src, dst, ss, rs, to):
        return pltpu.make_async_remote_copy(
            src_ref=src, dst_ref=dst, send_sem=ss, recv_sem=rs,
            device_id={axis: to}, device_id_type=pl.DeviceIdType.MESH)

    def halo(which, p):
        src = (kw_h, v_h, qw_h, g_h)[which]
        dst = (kprev, vprev, qnext, gnext)[which]
        to = me + 1 if which < 2 else me - 1
        return remote(src.at[:, cut(p)], dst.at[:, cut(p)],
                      halo_s.at[which, p], halo_r.at[which, p], to)

    def f_copy(p):
        return remote(f_out.at[p], f_in.at[p], f_s.at[p], f_r.at[p], me + 1)

    def b_copy(p):
        return remote(b_out.at[p], b_in.at[p], b_s.at[p], b_r.at[p], me - 1)

    def n_copy(to):
        return remote(nown, nall.at[me], n_s.at[to], n_r.at[me], to)

    def nb_copy(to):
        return remote(nbown, nball.at[me], nb_s.at[to], nb_r.at[me], to)

    def n_from(j):
        return remote(nown, nall.at[j], n_s.at[j], n_r.at[j], j)

    def nb_from(j):
        return remote(nbown, nball.at[j], nb_s.at[j], nb_r.at[j], j)

    def stats_copy():
        return remote(stat_t, stat_in, st_s, st_r, me - 1)

    def loop(low, high, body):
        def one(i, c):
            body(i)
            return c
        lax.fori_loop(low, high, one, 0)

    barrier = pltpu.get_barrier_semaphore()
    for d in range(1, n):
        pl.semaphore_signal(barrier, inc=1, device_id={axis: lax.rem(me + d, n)},
                            device_id_type=pl.DeviceIdType.MESH)

    fetch = [pltpu.make_async_copy(a, b, in_s.at[i]) for i, (a, b) in enumerate(
        ((kl_h, kl), (v_h, v), (ql_h, ql), (g_h, g), (kw_h, kw), (qw_h, qw)))]
    for f in fetch:
        f.start()
    nown[...] = jnp.zeros_like(nown)
    nbown[...] = jnp.zeros_like(nbown)
    dden[...] = jnp.zeros_like(dden)
    stat[...] = jnp.zeros_like(stat)
    ones8 = jnp.ones((8, tok), BF)

    @pl.when(first)
    def _():
        kprev[...] = jnp.zeros_like(kprev)
        vprev[...] = jnp.zeros_like(vprev)
        f_in[...] = jnp.zeros_like(f_in)

    @pl.when(last)
    def _():
        qnext[...] = jnp.zeros_like(qnext)
        gnext[...] = jnp.zeros_like(gnext)
        stat_in[...] = jnp.zeros_like(stat_in)
        b_in[...] = jnp.zeros_like(b_in)

    fetch[0].wait()
    kt[...] = kl[...].astype(F32).T
    fetch[1].wait()

    def pair_features(x, query):
        return jnp.concatenate([features(x[:FD], query), features(x[FD:], query)], 0).astype(BF)

    def phase_a(p):
        feats = pair_features(kt[prow(p), :], False)
        kf[p] = feats
        nown[pl.ds(2 * p, 1), 0:NF] = dot(ones8, feats[:NF], 1, 1)[0:1]
        nown[pl.ds(2 * p + 1, 1), 0:NF] = dot(ones8, feats[NF:], 1, 1)[0:1]
        s_own[p] = pick(dot(feats, v[:, cut(p)], 1, 0))

    loop(0, pairs, phase_a)
    pl.semaphore_wait(barrier, n - 1)
    loop(me + 1, n, lambda j: n_copy(j).start())

    def send_front(p):
        @pl.when(jnp.logical_not(last))
        def _():
            halo(0, p).start()
            halo(1, p).start()

    def send_back(p):
        @pl.when(jnp.logical_not(first))
        def _():
            halo(2, p).start()
            halo(3, p).start()

    loop(0, pairs, send_front)
    fetch[2].wait()
    qt[...] = ql[...].astype(F32).T

    def spread_q(p):
        x = qt[prow(p), :].astype(BF)
        z = jnp.zeros((FD, tok), BF)
        return jnp.concatenate(
            [jnp.concatenate([x[:FD], z], 0), jnp.concatenate([z, x[FD:]], 0)], 1)

    def phase_b(p):
        qf[p] = pair_features(qt[prow(p), :], True)
        s = dot(spread_q(p), kt[prow(p), :].astype(BF), 0, 0) * 0.25
        kk = jnp.where(causal2, 1.0 + s + 0.5 * s * s, 0.0)
        kern[p] = kk.astype(BF)
        plus[p] = 1.0 + s
        ksum[p] = pick(jnp.broadcast_to(jnp.sum(kk, 1, keepdims=True), (2 * tok, 128)))

    loop(0, pairs, phase_b)

    def gathered(low, high, arrive, slots):
        def one(j, total):
            arrive(j).wait_recv()
            return total + slots[j]
        total = lax.fori_loop(low, high, one, jnp.zeros(nown.shape, F32))
        full = jnp.concatenate([total, jnp.zeros((128 - heads, nown.shape[1]), F32)], 0)
        return full.T[0:NF].astype(BF)

    ncol[...] = gathered(0, me, n_from, nall)
    fetch[3].wait()

    def phase_c(p):
        prior = []
        for hh in range(2):
            every = dot(qf[p, hh * NF : (hh + 1) * NF], ncol[...], 0, 0)
            prior.append(jnp.sum(jnp.where(lanes2 == 2 * p + hh, every, 0.0), 1, keepdims=True))
        r = 1.0 / (ksum[p] + jnp.where(lane < DH, prior[0], prior[1]))
        rden[p] = r
        low = (g[:, cut(p)].astype(F32) * r).astype(BF)
        dn[:, cut(p)] = low
        sb_own[p] = pick(dot(qf[p], low, 1, 0))

    loop(0, pairs, phase_c)
    fetch[4].wait()
    fetch[5].wait()

    def window(p):
        @pl.when(jnp.logical_not(first))
        def _():
            halo(0, p).wait_recv()
            halo(1, p).wait_recv()
        c = cut(p)
        k = jnp.concatenate([kw[:, c], kprev[:, c]], 0)
        vv = jnp.concatenate([v[:, c], vprev[:, c]], 0)
        qs, gs = both_halves(qw[:, c]), both_halves(g[:, c])
        prior = jnp.logical_and(cols > rows, me > 0)
        seen = jnp.concatenate([causal, prior], 1)
        seen = jnp.concatenate([seen, seen], 0)
        s = jnp.where(seen, dot(qs, k, 1, 1) * 0.125, -1e30)
        m = jnp.max(s, 1, keepdims=True)
        e = jnp.exp(s - m)
        total = jnp.sum(e, 1, keepdims=True)
        a = e * (1.0 / total)
        low = a.astype(BF)
        res = dot(low, vv, 1, 0)
        inner = jnp.sum(gs.astype(F32) * res, 1, keepdims=True)
        ds = (a * (dot(gs, vv, 1, 1) - inner)).astype(BF)
        win[:, c] = pick(res)
        gqw[:, c] = (pick(dot(ds, k, 1, 0)) * 0.125).astype(BF)
        dwk[:, c] = dot(ds[:, :tok], qs, 0, 0)
        dwv[:, c] = dot(low[:, :tok], gs, 0, 0)
        logsum = m + jnp.log(total)
        old = stat[...]
        for hh in range(2):
            part = slice(hh * tok, (hh + 1) * tok)
            old = jnp.where(lanes2 == 2 * p + hh, logsum[part], old)
            old = jnp.where(lanes2 == heads + 2 * p + hh, inner[part], old)
        stat[...] = old

    def f_step(p):
        @pl.when(jnp.logical_not(first))
        def _():
            f_copy(p).wait_recv()

        @pl.when(jnp.logical_not(last))
        def _():
            f_out[p] = (f_in[p].astype(F32) + s_own[p]).astype(BF)
            f_copy(p).start()

    def b_step(p):
        @pl.when(jnp.logical_not(last))
        def _():
            b_copy(p).wait_recv()

        @pl.when(jnp.logical_not(first))
        def _():
            b_out[p] = (b_in[p].astype(F32) + sb_own[p]).astype(BF)
            b_copy(p).start()

    def phase_d(p):
        c = cut(p)
        vv, r, pre = v[:, c], rden[p], f_in[p]
        num = dot(kern[p], vv, 1, 0)
        num = jnp.where(lane < DH, num[:tok] + dot(qf[p, :NF], pre, 0, 0),
                        num[tok:] + dot(qf[p, NF:], pre, 0, 0))
        out = num * r
        mixed[:, c] = (out + win[:, c]).astype(BF)
        prod = g[:, c].astype(F32) * out * r
        zero = jnp.zeros_like(prod)
        dd = -jnp.sum(jnp.concatenate(
            [jnp.where(lane < DH, prod, zero), jnp.where(lane < DH, zero, prod)], 0), 1, keepdims=True)
        one_head = [jnp.where(lanes2 == 2 * p + hh, dd[hh * tok : (hh + 1) * tok], 0.0) for hh in range(2)]
        dden[...] += one_head[0] + one_head[1]
        dm = both_halves(dn[:, c])
        ds = jnp.where(causal2, dot(dm, vv, 1, 1) + dd, 0.0) * plus[p]
        ds = ds.astype(BF)
        d_feat = dot(jnp.concatenate([pre, ncol[...]], 1),
                     jnp.concatenate([dm, jnp.concatenate(one_head, 0).astype(BF)], 1), 1, 1)
        x = qt[prow(p), :]
        dq = dot(kt[prow(p), :].astype(BF), ds, 1, 1) * 0.25
        dqt[prow(p), :] = jnp.concatenate(
            [dq[:FD, :tok] + pull(x[:FD], d_feat[:, :tok], True),
             dq[FD:, tok:] + pull(x[FD:], d_feat[:, tok:], True)], 0)
        dkt[prow(p), :] = dot(spread_q(p), ds, 1, 0) * 0.25

    def wave(j):
        fp = j - me

        @pl.when(jnp.logical_and(fp >= 0, fp < pairs))
        def _():
            f_step(fp)
        bp = j - (n - 1 - me)

        @pl.when(jnp.logical_and(bp >= 0, bp < pairs))
        def _():
            b_step(bp)

        @pl.when(j < pairs)
        def _():
            send_back(j)
            window(j)

        @pl.when(j == pairs - 1)
        def _():
            stat_t[...] = stat[...].T[0 : 2 * heads]

            @pl.when(jnp.logical_not(first))
            def _():
                stats_copy().start()

        @pl.when(j >= n - 1)
        def _():
            phase_d(j - (n - 1))

    loop(0, pairs + n - 1, wave)
    dden[...] = dden[...].T

    def back_norm(h):
        one = jnp.broadcast_to(dden[pl.ds(h, 1), :], (8, tok)).astype(BF)
        feats = qf[h // 2, pl.ds(pl.multiple_of(lax.rem(h, 2) * NF, 16), NF), :]
        nbown[pl.ds(h, 1), 0:NF] = dot(one, feats, 1, 1)[0:1]

    loop(0, heads, back_norm)
    loop(0, me, lambda j: nb_copy(j).start())
    gql[...] = dqt[...].T.astype(BF)

    @pl.when(jnp.logical_not(last))
    def _():
        stats_copy().wait_recv()

    def key_side(p):
        @pl.when(jnp.logical_not(last))
        def _():
            halo(2, p).wait_recv()
            halo(3, p).wait_recv()
        c = cut(p)
        q, gg = qnext[:, c], gnext[:, c]
        live = jnp.logical_and(rows > cols, me < n - 1)
        s = dot(both_halves(kw[:, c]), q, 1, 1) * 0.125
        da = dot(both_halves(v[:, c]), gg, 1, 1)
        aa, dd = [], []
        for hh in range(2):
            part = slice(hh * tok, (hh + 1) * tok)
            h = 2 * p + hh
            a = jnp.exp(jnp.where(live, s[part] - stat_in[pl.ds(h, 1), :], -1e30))
            aa.append(a.astype(BF))
            dd.append((a * (da[part] - stat_in[pl.ds(heads + h, 1), :])).astype(BF))
        dk = dot(jnp.concatenate(dd, 1), both_halves(q), 1, 0)
        gkw[:, c] = ((dwk[:, c] + dk) * 0.125).astype(BF)
        dwv[:, c] += dot(jnp.concatenate(aa, 1), both_halves(gg), 1, 0)

    loop(0, pairs, key_side)
    nbcol[...] = gathered(me + 1, n, nb_from, nball)

    def phase_e(p):
        c = cut(p)
        vv, post = v[:, c], b_in[p]
        dv = dot(kern[p], both_halves(dn[:, c]), 0, 0) + dot(kf[p], both_halves(post), 0, 0)
        gv[:, c] = (dv + dwv[:, c]).astype(BF)
        one_head = [jnp.where(lanes2 == 2 * p + hh, 1.0, 0.0).astype(BF) for hh in range(2)]
        d_feat = dot(jnp.concatenate([post, nbcol[...]], 1),
                     jnp.concatenate([both_halves(vv), jnp.concatenate(one_head, 0)], 1), 1, 1)
        x = kt[prow(p), :]
        dkt[prow(p), :] += jnp.concatenate(
            [pull(x[:FD], d_feat[:, :tok], False), pull(x[FD:], d_feat[:, tok:], False)], 0)

    loop(0, pairs, phase_e)
    gkl[...] = dkt[...].T.astype(BF)

    def drain(p):
        @pl.when(jnp.logical_not(last))
        def _():
            halo(0, p).wait_send()
            halo(1, p).wait_send()
            f_copy(p).wait_send()

        @pl.when(jnp.logical_not(first))
        def _():
            halo(2, p).wait_send()
            halo(3, p).wait_send()
            b_copy(p).wait_send()

    loop(0, pairs, drain)
    loop(me + 1, n, lambda j: n_copy(j).wait_send())
    loop(0, me, lambda j: nb_copy(j).wait_send())

    @pl.when(jnp.logical_not(first))
    def _():
        stats_copy().wait_send()


def writer(*refs):
    count = 6
    held, load_s, store_s = refs[2 * count : 3 * count], refs[-2], refs[-1]
    loads = [pltpu.make_async_copy(refs[i], held[i], load_s.at[i]) for i in range(count)]
    stores = [pltpu.make_async_copy(held[i], refs[count + i], store_s.at[i]) for i in range(count)]
    for c in loads:
        c.start()
    for c, d in zip(loads, stores):
        c.wait()
        d.start()
    for d in stores:
        d.wait()


def local(n, axis, *args):
    ql, v = args[0], args[4]
    tok, width = v.shape
    lin = ql.shape[1]
    pairs = width // 128
    heads = 2 * pairs
    vm = pltpu.VMEM
    dma = pltpu.SemaphoreType.DMA
    state16 = vm((pairs, NF, 128), BF)
    state32 = vm((pairs, NF, 128), F32)
    rows = vm((heads, 256), F32)
    wide32 = vm((tok, width), F32)
    wide16 = vm((tok, width), BF)
    lin16 = vm((tok, lin), BF)
    lin32 = vm((lin, tok), F32)
    tile32 = vm((pairs, tok, 128), F32)
    feats = vm((pairs, 2 * NF, tok), BF)
    small = vm((tok, 128), F32)
    scratch = [
        lin16, lin16, wide16, wide16, wide16, wide16,
        lin32, lin32, feats, feats, vm((pairs, 2 * tok, tok), BF), vm((pairs, 2 * tok, tok), F32), tile32,
        rows, vm((n, heads, 256), F32), vm((NF, 128), BF), state32, state16, state16,
        state32, state16, state16, tile32, wide16, wide32, wide32, wide32,
        small, small, vm((2 * heads, tok), F32), vm((2 * heads, tok), F32),
        rows, vm((n, heads, 256), F32), vm((NF, 128), BF),
        wide16, wide16, wide16, wide16, lin32, lin32,
        dma((6,)), dma((4, pairs)), dma((4, pairs)), dma((n,)), dma((n,)), dma((n,)), dma((n,)),
        dma((pairs,)), dma((pairs,)), dma((pairs,)), dma((pairs,)), dma, dma,
    ]
    order = (v, ql, ql, v, v, v)
    shapes = tuple(jax.ShapeDtypeStruct(a.shape, BF) for a in order)
    hbm = pl.BlockSpec(memory_space=pltpu.HBM)
    anywhere = pl.BlockSpec(memory_space=pl.ANY)
    made = pl.pallas_call(
        functools.partial(kernel, n, axis),
        out_shape=shapes,
        in_specs=[hbm] * 6,
        out_specs=tuple([pl.BlockSpec(memory_space=pltpu.VMEM)] * 6),
        scratch_shapes=scratch,
        compiler_params=pltpu.CompilerParams(
            collective_id=0, has_side_effects=True, vmem_limit_bytes=60 * 1024 * 1024),
    )(*args)
    return pl.pallas_call(
        writer,
        out_shape=shapes,
        in_specs=[anywhere] * 6,
        out_specs=tuple([anywhere] * 6),
        scratch_shapes=[vm(a.shape, BF) for a in order] + [dma((6,)), dma((6,))],
        compiler_params=pltpu.CompilerParams(vmem_limit_bytes=60 * 1024 * 1024),
    )(*made)


def solution(mesh):
    place = P(("dp", "seq"), None)
    return jax.shard_map(
        functools.partial(local, mesh.shape["seq"], "seq"),
        mesh=mesh,
        in_specs=(place,) * 6,
        out_specs=(place,) * 6,
        check_vma=False,
    )
```

```python
import functools

import jax
import jax.numpy as jnp
from jax import lax
from jax.experimental import pallas as pl
from jax.experimental.pallas import tpu as pltpu
from jax.sharding import PartitionSpec as P

FD = 16
DH = 64
NF = 160
F32 = jnp.float32
BF = jnp.bfloat16


def dot(a, b, ca, cb):
    return lax.dot_general(a, b, (((ca,), (cb,)), ((), ())), preferred_element_type=F32)


def turned(x, d):
    return x if d == 0 else jnp.concatenate([x[d:], x[:d]], 0)


def features(x, query):
    pair = 1.0 / 16.0 if query else 1.0
    parts = [x * x * (pair * 0.5 if query else 1.0)]
    scaled = x * pair
    for d in range(1, 8):
        parts.append(scaled * turned(x, d))
    parts.append(scaled[:8] * x[8:])
    parts.append(x * 0.25 if query else x)
    row = lax.broadcasted_iota(jnp.int32, (8, x.shape[1]), 0)
    parts.append(jnp.where(row == 0, 1.0, 0.0).astype(F32))
    return jnp.concatenate(parts, 0)


def pull(x, d_feat, query):
    pair = 1.0 / 16.0 if query else 1.0
    total = d_feat[0:16] * x * (pair if query else 2.0)
    cross = jnp.zeros_like(x)
    for d in range(1, 8):
        part = d_feat[16 * d : 16 * d + 16]
        cross = cross + part * turned(x, d) + turned(part * x, 16 - d)
    last = d_feat[128:136]
    cross = cross + jnp.concatenate([last * x[8:], last * x[:8]], 0)
    line = d_feat[136:152]
    return total + cross * pair + line * (0.25 if query else 1.0)


def kernel(n, axis, ql_h, kl_h, qw_h, kw_h, v_h, g_h, mixed, gql, gkl, gqw, gkw, gv,
           ql, kl, qw, kw, v, g,
           qt, kt, qf, kf, kern, plus, ksum, nown, nall, ncol, s_own, f_in, f_out,
           sb_own, b_in, b_out, rden, dn, win, dwk, dwv, dden, stat, stat_t, stat_in,
           nbown, nball, nbcol, kprev, vprev, qnext, gnext, dqt, dkt,
           in_s, halo_s, halo_r, n_s, n_r, nb_s, nb_r, f_s, f_r, b_s, b_r, st_s, st_r):
    me = lax.axis_index(axis)
    tok = ql.shape[0]
    pairs = v.shape[1] // 128
    heads = 2 * pairs
    first, last = me == 0, me == n - 1
    lane = lax.broadcasted_iota(jnp.int32, (1, 128), 1)
    half = [(lane < DH).astype(F32).astype(BF), (lane >= DH).astype(F32).astype(BF)]
    rows = lax.broadcasted_iota(jnp.int32, (tok, tok), 0)
    cols = lax.broadcasted_iota(jnp.int32, (tok, tok), 1)
    lanes2 = lax.broadcasted_iota(jnp.int32, (tok, 128), 1)
    causal = cols <= rows
    causal2 = jnp.concatenate([causal, causal], 0)

    def cut(p):
        return pl.ds(pl.multiple_of(p * 128, 128), 128)

    def prow(p):
        return pl.ds(pl.multiple_of(p * 2 * FD, 2 * FD), 2 * FD)

    def both_halves(x):
        return jnp.concatenate([x * half[0], x * half[1]], 0)

    def pick(x):
        m = x.shape[0] // 2
        return jnp.where(lane < DH, x[:m], x[m:])

    def remote(src, dst, ss, rs, to):
        return pltpu.make_async_remote_copy(
            src_ref=src, dst_ref=dst, send_sem=ss, recv_sem=rs,
            device_id={axis: to}, device_id_type=pl.DeviceIdType.MESH)

    def halo(which, p):
        src = (kw_h, v_h, qw_h, g_h)[which]
        dst = (kprev, vprev, qnext, gnext)[which]
        to = me + 1 if which < 2 else me - 1
        return remote(src.at[:, cut(p)], dst.at[:, cut(p)],
                      halo_s.at[which, p], halo_r.at[which, p], to)

    def f_copy(p):
        return remote(f_out.at[p], f_in.at[p], f_s.at[p], f_r.at[p], me + 1)

    def b_copy(p):
        return remote(b_out.at[p], b_in.at[p], b_s.at[p], b_r.at[p], me - 1)

    def n_copy(to):
        return remote(nown, nall.at[me], n_s.at[to], n_r.at[me], to)

    def nb_copy(to):
        return remote(nbown, nball.at[me], nb_s.at[to], nb_r.at[me], to)

    def n_from(j):
        return remote(nown, nall.at[j], n_s.at[j], n_r.at[j], j)

    def nb_from(j):
        return remote(nbown, nball.at[j], nb_s.at[j], nb_r.at[j], j)

    def stats_copy():
        return remote(stat_t, stat_in, st_s, st_r, me - 1)

    def loop(low, high, body):
        def one(i, c):
            body(i)
            return c
        lax.fori_loop(low, high, one, 0)

    barrier = pltpu.get_barrier_semaphore()
    for d in range(1, n):
        pl.semaphore_signal(barrier, inc=1, device_id={axis: lax.rem(me + d, n)},
                            device_id_type=pl.DeviceIdType.MESH)

    fetch = [pltpu.make_async_copy(a, b, in_s.at[i]) for i, (a, b) in enumerate(
        ((kl_h, kl), (v_h, v), (ql_h, ql), (g_h, g), (kw_h, kw), (qw_h, qw)))]
    for f in fetch:
        f.start()
    nown[...] = jnp.zeros_like(nown)
    nbown[...] = jnp.zeros_like(nbown)
    dden[...] = jnp.zeros_like(dden)
    stat[...] = jnp.zeros_like(stat)
    ones8 = jnp.ones((8, tok), BF)

    @pl.when(first)
    def _():
        kprev[...] = jnp.zeros_like(kprev)
        vprev[...] = jnp.zeros_like(vprev)
        f_in[...] = jnp.zeros_like(f_in)

    @pl.when(last)
    def _():
        qnext[...] = jnp.zeros_like(qnext)
        gnext[...] = jnp.zeros_like(gnext)
        stat_in[...] = jnp.zeros_like(stat_in)
        b_in[...] = jnp.zeros_like(b_in)

    def send_front(p):
        @pl.when(jnp.logical_not(last))
        def _():
            halo(0, p).start()
            halo(1, p).start()

    def send_back(p):
        @pl.when(jnp.logical_not(first))
        def _():
            halo(2, p).start()
            halo(3, p).start()

    pl.semaphore_wait(barrier, n - 1)
    early = 2
    loop(0, early, send_front)
    fetch[0].wait()
    kt[...] = kl[...].astype(F32).T
    fetch[1].wait()

    def pair_features(x, query):
        return jnp.concatenate([features(x[:FD], query), features(x[FD:], query)], 0).astype(BF)

    def phase_a(p):
        feats = pair_features(kt[prow(p), :], False)
        kf[p] = feats
        nown[pl.ds(2 * p, 1), 0:NF] = dot(ones8, feats[:NF], 1, 1)[0:1]
        nown[pl.ds(2 * p + 1, 1), 0:NF] = dot(ones8, feats[NF:], 1, 1)[0:1]
        s_own[p] = pick(dot(feats, v[:, cut(p)], 1, 0))

    loop(0, pairs, phase_a)
    loop(me + 1, n, lambda j: n_copy(j).start())

    fetch[2].wait()
    qt[...] = ql[...].astype(F32).T

    def spread_q(p):
        x = qt[prow(p), :].astype(BF)
        z = jnp.zeros((FD, tok), BF)
        return jnp.concatenate(
            [jnp.concatenate([x[:FD], z], 0), jnp.concatenate([z, x[FD:]], 0)], 1)

    def f_step(p):
        @pl.when(jnp.logical_not(first))
        def _():
            f_copy(p).wait_recv()

        @pl.when(jnp.logical_not(last))
        def _():
            f_out[p] = (f_in[p].astype(F32) + s_own[p]).astype(BF)
            f_copy(p).start()

    def b_step(p):
        @pl.when(jnp.logical_not(last))
        def _():
            b_copy(p).wait_recv()

        @pl.when(jnp.logical_not(first))
        def _():
            b_out[p] = (b_in[p].astype(F32) + sb_own[p]).astype(BF)
            b_copy(p).start()

    def f_wave(t):
        p = t - me

        @pl.when(jnp.logical_and(p >= 0, p < pairs))
        def _():
            f_step(p)

    def phase_b(p):
        f_wave(p)

        @pl.when(p + early < pairs)
        def _():
            send_front(p + early)
        qf[p] = pair_features(qt[prow(p), :], True)
        s = dot(spread_q(p), kt[prow(p), :].astype(BF), 0, 0) * 0.25
        kk = jnp.where(causal2, 1.0 + s + 0.5 * s * s, 0.0)
        kern[p] = kk.astype(BF)
        plus[p] = 1.0 + s
        ksum[p] = pick(jnp.broadcast_to(jnp.sum(kk, 1, keepdims=True), (2 * tok, 128)))

    loop(0, pairs, phase_b)

    def gathered(low, high, arrive, slots):
        def one(j, total):
            arrive(j).wait_recv()
            return total + slots[j]
        total = lax.fori_loop(low, high, one, jnp.zeros(nown.shape, F32))
        full = jnp.concatenate([total, jnp.zeros((128 - heads, nown.shape[1]), F32)], 0)
        return full.T[0:NF].astype(BF)

    ncol[...] = gathered(0, me, n_from, nall)
    fetch[3].wait()

    def phase_c(p):
        f_wave(pairs + p)
        send_back(p)
        prior = []
        for hh in range(2):
            every = dot(qf[p, hh * NF : (hh + 1) * NF], ncol[...], 0, 0)
            prior.append(jnp.sum(jnp.where(lanes2 == 2 * p + hh, every, 0.0), 1, keepdims=True))
        r = 1.0 / (ksum[p] + jnp.where(lane < DH, prior[0], prior[1]))
        rden[p] = r
        low = (g[:, cut(p)].astype(F32) * r).astype(BF)
        dn[:, cut(p)] = low
        sb_own[p] = pick(dot(qf[p], low, 1, 0))

    loop(0, pairs, phase_c)
    loop(2 * pairs, pairs + n - 1, f_wave)
    fetch[4].wait()
    fetch[5].wait()

    def window(p):
        @pl.when(jnp.logical_not(first))
        def _():
            halo(0, p).wait_recv()
            halo(1, p).wait_recv()
        c = cut(p)
        k = jnp.concatenate([kw[:, c], kprev[:, c]], 0)
        vv = jnp.concatenate([v[:, c], vprev[:, c]], 0)
        qs, gs = both_halves(qw[:, c]), both_halves(g[:, c])
        prior = jnp.logical_and(cols > rows, me > 0)
        seen = jnp.concatenate([causal, prior], 1)
        seen = jnp.concatenate([seen, seen], 0)
        s = jnp.where(seen, dot(qs, k, 1, 1) * 0.125, -1e30)
        m = jnp.max(s, 1, keepdims=True)
        e = jnp.exp(s - m)
        total = jnp.sum(e, 1, keepdims=True)
        a = e * (1.0 / total)
        low = a.astype(BF)
        res = dot(low, vv, 1, 0)
        inner = jnp.sum(gs.astype(F32) * res, 1, keepdims=True)
        ds = (a * (dot(gs, vv, 1, 1) - inner)).astype(BF)
        win[:, c] = pick(res)
        gqw[:, c] = (pick(dot(ds, k, 1, 0)) * 0.125).astype(BF)
        dwk[:, c] = dot(ds[:, :tok], qs, 0, 0)
        dwv[:, c] = dot(low[:, :tok], gs, 0, 0)
        logsum = m + jnp.log(total)
        old = stat[...]
        for hh in range(2):
            part = slice(hh * tok, (hh + 1) * tok)
            old = jnp.where(lanes2 == 2 * p + hh, logsum[part], old)
            old = jnp.where(lanes2 == heads + 2 * p + hh, inner[part], old)
        stat[...] = old

    def phase_d(p):
        c = cut(p)
        vv, r, pre = v[:, c], rden[p], f_in[p]
        num = dot(kern[p], vv, 1, 0)
        num = jnp.where(lane < DH, num[:tok] + dot(qf[p, :NF], pre, 0, 0),
                        num[tok:] + dot(qf[p, NF:], pre, 0, 0))
        out = num * r
        mixed[:, c] = (out + win[:, c]).astype(BF)
        prod = g[:, c].astype(F32) * out * r
        zero = jnp.zeros_like(prod)
        dd = -jnp.sum(jnp.concatenate(
            [jnp.where(lane < DH, prod, zero), jnp.where(lane < DH, zero, prod)], 0), 1, keepdims=True)
        one_head = [jnp.where(lanes2 == 2 * p + hh, dd[hh * tok : (hh + 1) * tok], 0.0) for hh in range(2)]
        dden[...] += one_head[0] + one_head[1]
        dm = both_halves(dn[:, c])
        ds = jnp.where(causal2, dot(dm, vv, 1, 1) + dd, 0.0) * plus[p]
        ds = ds.astype(BF)
        d_feat = dot(jnp.concatenate([pre, ncol[...]], 1),
                     jnp.concatenate([dm, jnp.concatenate(one_head, 0).astype(BF)], 1), 1, 1)
        x = qt[prow(p), :]
        dq = dot(kt[prow(p), :].astype(BF), ds, 1, 1) * 0.25
        dqt[prow(p), :] = jnp.concatenate(
            [dq[:FD, :tok] + pull(x[:FD], d_feat[:, :tok], True),
             dq[FD:, tok:] + pull(x[FD:], d_feat[:, tok:], True)], 0)
        dkt[prow(p), :] = dot(spread_q(p), ds, 1, 0) * 0.25

    def key_side(p):
        @pl.when(jnp.logical_not(last))
        def _():
            halo(2, p).wait_recv()
            halo(3, p).wait_recv()
        c = cut(p)
        q, gg = qnext[:, c], gnext[:, c]
        live = jnp.logical_and(rows > cols, me < n - 1)
        s = dot(both_halves(kw[:, c]), q, 1, 1) * 0.125
        da = dot(both_halves(v[:, c]), gg, 1, 1)
        aa, dd = [], []
        for hh in range(2):
            part = slice(hh * tok, (hh + 1) * tok)
            h = 2 * p + hh
            a = jnp.exp(jnp.where(live, s[part] - stat_in[pl.ds(h, 1), :], -1e30))
            aa.append(a.astype(BF))
            dd.append((a * (da[part] - stat_in[pl.ds(heads + h, 1), :])).astype(BF))
        dk = dot(jnp.concatenate(dd, 1), both_halves(q), 1, 0)
        gkw[:, c] = ((dwk[:, c] + dk) * 0.125).astype(BF)
        dwv[:, c] += dot(jnp.concatenate(aa, 1), both_halves(gg), 1, 0)

    def phase_e(p):
        c = cut(p)
        vv, post = v[:, c], b_in[p]
        dv = dot(kern[p], both_halves(dn[:, c]), 0, 0) + dot(kf[p], both_halves(post), 0, 0)
        gv[:, c] = (dv + dwv[:, c]).astype(BF)
        one_head = [jnp.where(lanes2 == 2 * p + hh, 1.0, 0.0).astype(BF) for hh in range(2)]
        d_feat = dot(jnp.concatenate([post, nbcol[...]], 1),
                     jnp.concatenate([both_halves(vv), jnp.concatenate(one_head, 0)], 1), 1, 1)
        x = kt[prow(p), :]
        dkt[prow(p), :] += jnp.concatenate(
            [pull(x[:FD], d_feat[:, :tok], False), pull(x[FD:], d_feat[:, tok:], False)], 0)

    def back_norm(h):
        one = jnp.broadcast_to(dden[pl.ds(h, 1), :], (8, tok)).astype(BF)
        feats = qf[h // 2, pl.ds(pl.multiple_of(lax.rem(h, 2) * NF, 16), NF), :]
        nbown[pl.ds(h, 1), 0:NF] = dot(one, feats, 1, 1)[0:1]

    turns = pairs + n - 1
    key_at = pairs
    e_at = max(pairs, n - 1) + 1

    def wave(j):
        bp = j - (n - 1 - me)

        @pl.when(jnp.logical_and(bp >= 0, bp < pairs))
        def _():
            b_step(bp)

        @pl.when(j < pairs)
        def _():
            window(j)
            phase_d(j)

        @pl.when(j == pairs - 1)
        def _():
            stat_t[...] = stat[...].T[0 : 2 * heads]

            @pl.when(jnp.logical_not(first))
            def _():
                stats_copy().start()
            dden[...] = dden[...].T
            loop(0, heads, back_norm)
            loop(0, me, lambda i: nb_copy(i).start())

        @pl.when(j == key_at)
        def _():
            @pl.when(jnp.logical_not(last))
            def _():
                stats_copy().wait_recv()

        @pl.when(jnp.logical_and(j >= key_at, j < key_at + pairs))
        def _():
            key_side(j - key_at)

        @pl.when(j == e_at)
        def _():
            nbcol[...] = gathered(me + 1, n, nb_from, nball)

        @pl.when(jnp.logical_and(j >= e_at, j < e_at + pairs))
        def _():
            phase_e(j - e_at)

    loop(0, max(turns, key_at + pairs, e_at + pairs), wave)
    gql[...] = dqt[...].T.astype(BF)
    gkl[...] = dkt[...].T.astype(BF)

    def drain(p):
        @pl.when(jnp.logical_not(last))
        def _():
            halo(0, p).wait_send()
            halo(1, p).wait_send()
            f_copy(p).wait_send()

        @pl.when(jnp.logical_not(first))
        def _():
            halo(2, p).wait_send()
            halo(3, p).wait_send()
            b_copy(p).wait_send()

    loop(0, pairs, drain)
    loop(me + 1, n, lambda j: n_copy(j).wait_send())
    loop(0, me, lambda j: nb_copy(j).wait_send())

    @pl.when(jnp.logical_not(first))
    def _():
        stats_copy().wait_send()


def writer(*refs):
    count = 6
    held, load_s, store_s = refs[2 * count : 3 * count], refs[-2], refs[-1]
    loads = [pltpu.make_async_copy(refs[i], held[i], load_s.at[i]) for i in range(count)]
    stores = [pltpu.make_async_copy(held[i], refs[count + i], store_s.at[i]) for i in range(count)]
    for c in loads:
        c.start()
    for c, d in zip(loads, stores):
        c.wait()
        d.start()
    for d in stores:
        d.wait()


def local(n, axis, *args):
    ql, v = args[0], args[4]
    tok, width = v.shape
    lin = ql.shape[1]
    pairs = width // 128
    heads = 2 * pairs
    vm = pltpu.VMEM
    dma = pltpu.SemaphoreType.DMA
    state16 = vm((pairs, NF, 128), BF)
    state32 = vm((pairs, NF, 128), F32)
    rows = vm((heads, 256), F32)
    wide32 = vm((tok, width), F32)
    wide16 = vm((tok, width), BF)
    lin16 = vm((tok, lin), BF)
    lin32 = vm((lin, tok), F32)
    tile32 = vm((pairs, tok, 128), F32)
    feats = vm((pairs, 2 * NF, tok), BF)
    small = vm((tok, 128), F32)
    scratch = [
        lin16, lin16, wide16, wide16, wide16, wide16,
        lin32, lin32, feats, feats, vm((pairs, 2 * tok, tok), BF), vm((pairs, 2 * tok, tok), F32), tile32,
        rows, vm((n, heads, 256), F32), vm((NF, 128), BF), state32, state16, state16,
        state32, state16, state16, tile32, wide16, wide32, wide32, wide32,
        small, small, vm((2 * heads, tok), F32), vm((2 * heads, tok), F32),
        rows, vm((n, heads, 256), F32), vm((NF, 128), BF),
        wide16, wide16, wide16, wide16, lin32, lin32,
        dma((6,)), dma((4, pairs)), dma((4, pairs)), dma((n,)), dma((n,)), dma((n,)), dma((n,)),
        dma((pairs,)), dma((pairs,)), dma((pairs,)), dma((pairs,)), dma, dma,
    ]
    order = (v, ql, ql, v, v, v)
    shapes = tuple(jax.ShapeDtypeStruct(a.shape, BF) for a in order)
    hbm = pl.BlockSpec(memory_space=pltpu.HBM)
    anywhere = pl.BlockSpec(memory_space=pl.ANY)
    made = pl.pallas_call(
        functools.partial(kernel, n, axis),
        out_shape=shapes,
        in_specs=[hbm] * 6,
        out_specs=tuple([pl.BlockSpec(memory_space=pltpu.VMEM)] * 6),
        scratch_shapes=scratch,
        compiler_params=pltpu.CompilerParams(
            collective_id=0, has_side_effects=True, vmem_limit_bytes=60 * 1024 * 1024),
    )(*args)
    return pl.pallas_call(
        writer,
        out_shape=shapes,
        in_specs=[anywhere] * 6,
        out_specs=tuple([anywhere] * 6),
        scratch_shapes=[vm(a.shape, BF) for a in order] + [dma((6,)), dma((6,))],
        compiler_params=pltpu.CompilerParams(vmem_limit_bytes=60 * 1024 * 1024),
    )(*made)


def solution(mesh):
    place = P(("dp", "seq"), None)
    return jax.shard_map(
        functools.partial(local, mesh.shape["seq"], "seq"),
        mesh=mesh,
        in_specs=(place,) * 6,
        out_specs=(place,) * 6,
        check_vma=False,
    )
```

```python
import functools

import jax
import jax.numpy as jnp
from jax import lax
from jax.experimental import pallas as pl
from jax.experimental.pallas import tpu as pltpu
from jax.sharding import PartitionSpec as P

FD = 16
DH = 64
NF = 160
F32 = jnp.float32
BF = jnp.bfloat16


def dot(a, b, ca, cb):
    return lax.dot_general(a, b, (((ca,), (cb,)), ((), ())), preferred_element_type=F32)


def turned(x, d):
    return x if d == 0 else jnp.concatenate([x[d:], x[:d]], 0)


def features(x, query):
    pair = 1.0 / 16.0 if query else 1.0
    parts = [x * x * (pair * 0.5 if query else 1.0)]
    scaled = x * pair
    for d in range(1, 8):
        parts.append(scaled * turned(x, d))
    parts.append(scaled[:8] * x[8:])
    parts.append(x * 0.25 if query else x)
    row = lax.broadcasted_iota(jnp.int32, (8, x.shape[1]), 0)
    parts.append(jnp.where(row == 0, 1.0, 0.0).astype(F32))
    return jnp.concatenate(parts, 0)


def pull(x, d_feat, query):
    pair = 1.0 / 16.0 if query else 1.0
    total = d_feat[0:16] * x * (pair if query else 2.0)
    cross = jnp.zeros_like(x)
    for d in range(1, 8):
        part = d_feat[16 * d : 16 * d + 16]
        cross = cross + part * turned(x, d) + turned(part * x, 16 - d)
    last = d_feat[128:136]
    cross = cross + jnp.concatenate([last * x[8:], last * x[:8]], 0)
    line = d_feat[136:152]
    return total + cross * pair + line * (0.25 if query else 1.0)


def kernel(n, axis, ql_h, kl_h, qw_h, kw_h, v_h, g_h, mixed, gql, gkl, gqw, gkw, gv,
           ql, kl, qw, kw, v, g,
           bias, later, tri, qt, kt, qf, kf, kern, plus, ksum, nown, nall, ncol, s_own, f_in, f_out,
           sb_own, b_in, b_out, rden, dn, win, dwk, dwv, dden, stat, stat_t, stat_in,
           nbown, nball, nbcol, kprev, vprev, qnext, gnext, dqt, dkt,
           in_s, halo_s, halo_r, n_s, n_r, nb_s, nb_r, f_s, f_r, b_s, b_r, st_s, st_r):
    me = lax.axis_index(axis)
    tok = ql.shape[0]
    pairs = v.shape[1] // 128
    heads = 2 * pairs
    first, last = me == 0, me == n - 1
    lane = lax.broadcasted_iota(jnp.int32, (1, 128), 1)
    half = [(lane < DH).astype(F32).astype(BF), (lane >= DH).astype(F32).astype(BF)]
    rows = lax.broadcasted_iota(jnp.int32, (tok, tok), 0)
    cols = lax.broadcasted_iota(jnp.int32, (tok, tok), 1)
    lanes2 = lax.broadcasted_iota(jnp.int32, (tok, 128), 1)
    causal = cols <= rows

    def cut(p):
        return pl.ds(pl.multiple_of(p * 128, 128), 128)

    def prow(p):
        return pl.ds(pl.multiple_of(p * 2 * FD, 2 * FD), 2 * FD)

    def both_halves(x, scale=None):
        if scale is not None:
            x = x * jnp.asarray(scale, BF)
        return jnp.concatenate([x * half[0], x * half[1]], 0)

    def pick(x):
        m = x.shape[0] // 2
        return jnp.where(lane < DH, x[:m], x[m:])

    def remote(src, dst, ss, rs, to):
        return pltpu.make_async_remote_copy(
            src_ref=src, dst_ref=dst, send_sem=ss, recv_sem=rs,
            device_id={axis: to}, device_id_type=pl.DeviceIdType.MESH)

    def halo(which, p):
        src = (kw_h, v_h, qw_h, g_h)[which]
        dst = (kprev, vprev, qnext, gnext)[which]
        to = me + 1 if which < 2 else me - 1
        return remote(src.at[:, cut(p)], dst.at[:, cut(p)],
                      halo_s.at[which, p], halo_r.at[which, p], to)

    def f_copy(p):
        return remote(f_out.at[p], f_in.at[p], f_s.at[p], f_r.at[p], me + 1)

    def b_copy(p):
        return remote(b_out.at[p], b_in.at[p], b_s.at[p], b_r.at[p], me - 1)

    def n_copy(to):
        return remote(nown, nall.at[me], n_s.at[to], n_r.at[me], to)

    def nb_copy(to):
        return remote(nbown, nball.at[me], nb_s.at[to], nb_r.at[me], to)

    def n_from(j):
        return remote(nown, nall.at[j], n_s.at[j], n_r.at[j], j)

    def nb_from(j):
        return remote(nbown, nball.at[j], nb_s.at[j], nb_r.at[j], j)

    def stats_copy():
        return remote(stat_t, stat_in, st_s, st_r, me - 1)

    def loop(low, high, body):
        def one(i, c):
            body(i)
            return c
        lax.fori_loop(low, high, one, 0)

    barrier = pltpu.get_barrier_semaphore()
    for d in range(1, n):
        pl.semaphore_signal(barrier, inc=1, device_id={axis: lax.rem(me + d, n)},
                            device_id_type=pl.DeviceIdType.MESH)

    fetch = [pltpu.make_async_copy(a, b, in_s.at[i]) for i, (a, b) in enumerate(
        ((kl_h, kl), (v_h, v), (ql_h, ql), (g_h, g), (kw_h, kw), (qw_h, qw)))]
    for f in fetch:
        f.start()
    nown[...] = jnp.zeros_like(nown)
    nbown[...] = jnp.zeros_like(nbown)
    dden[...] = jnp.zeros_like(dden)
    stat[...] = jnp.zeros_like(stat)
    ones8 = jnp.ones((8, tok), BF)
    never = jnp.full((tok, tok), -1e30, F32)
    none = jnp.zeros((tok, tok), F32)
    tri[...] = jnp.where(causal, 1.0, 0.0)
    bias[:, :tok] = jnp.where(causal, none, never)
    bias[:, tok:] = jnp.where(jnp.logical_and(cols > rows, me > 0), none, never)
    later[...] = jnp.where(jnp.logical_and(rows > cols, me < n - 1), none, never)
    dkt[...] = jnp.zeros_like(dkt)

    @pl.when(first)
    def _():
        kprev[...] = jnp.zeros_like(kprev)
        vprev[...] = jnp.zeros_like(vprev)
        f_in[...] = jnp.zeros_like(f_in)

    @pl.when(last)
    def _():
        qnext[...] = jnp.zeros_like(qnext)
        gnext[...] = jnp.zeros_like(gnext)
        stat_in[...] = jnp.zeros_like(stat_in)
        b_in[...] = jnp.zeros_like(b_in)

    fetch[0].wait()
    kt[...] = kl[...].astype(F32).T
    fetch[1].wait()

    def pair_features(x, query):
        return jnp.concatenate([features(x[:FD], query), features(x[FD:], query)], 0).astype(BF)

    def phase_a(p):
        feats = pair_features(kt[prow(p), :], False)
        kf[p] = feats
        nown[pl.ds(2 * p, 1), 0:NF] = dot(ones8, feats[:NF], 1, 1)[0:1]
        nown[pl.ds(2 * p + 1, 1), 0:NF] = dot(ones8, feats[NF:], 1, 1)[0:1]
        s_own[p] = pick(dot(feats, v[:, cut(p)], 1, 0))

    loop(0, pairs, phase_a)
    pl.semaphore_wait(barrier, n - 1)
    loop(me + 1, n, lambda j: n_copy(j).start())

    def send_front(p):
        @pl.when(jnp.logical_not(last))
        def _():
            halo(0, p).start()
            halo(1, p).start()

    def send_back(p):
        @pl.when(jnp.logical_not(first))
        def _():
            halo(2, p).start()
            halo(3, p).start()

    loop(0, pairs, send_front)
    fetch[2].wait()
    qt[...] = ql[...].astype(F32).T

    def spread_q(p):
        x = (qt[prow(p), :] * 0.25).astype(BF)
        z = jnp.zeros((FD, tok), BF)
        return jnp.concatenate(
            [jnp.concatenate([x[:FD], z], 0), jnp.concatenate([z, x[FD:]], 0)], 1)

    def phase_b(p):
        qf[p] = pair_features(qt[prow(p), :], True)
        s = dot(spread_q(p), kt[prow(p), :].astype(BF), 0, 0)
        mask = jnp.concatenate([tri[...], tri[...]], 0)
        kk = mask * (1.0 + s + 0.5 * s * s)
        kern[p] = kk.astype(BF)
        plus[p] = mask * (1.0 + s)
        ksum[p] = pick(jnp.broadcast_to(jnp.sum(kk, 1, keepdims=True), (2 * tok, 128)))

    loop(0, pairs, phase_b)

    def gathered(low, high, arrive, slots):
        def one(j, total):
            arrive(j).wait_recv()
            return total + slots[j]
        total = lax.fori_loop(low, high, one, jnp.zeros(nown.shape, F32))
        full = jnp.concatenate([total, jnp.zeros((128 - heads, nown.shape[1]), F32)], 0)
        return full.T[0:NF].astype(BF)

    ncol[...] = gathered(0, me, n_from, nall)
    fetch[3].wait()

    def phase_c(p):
        prior = []
        for hh in range(2):
            every = dot(qf[p, hh * NF : (hh + 1) * NF], ncol[...], 0, 0)
            prior.append(jnp.sum(jnp.where(lanes2 == 2 * p + hh, every, 0.0), 1, keepdims=True))
        r = 1.0 / (ksum[p] + jnp.where(lane < DH, prior[0], prior[1]))
        rden[p] = r
        low = (g[:, cut(p)].astype(F32) * r).astype(BF)
        dn[:, cut(p)] = low
        sb_own[p] = pick(dot(qf[p], low, 1, 0))

    loop(0, pairs, phase_c)
    fetch[4].wait()
    fetch[5].wait()

    def window(p):
        @pl.when(jnp.logical_not(first))
        def _():
            halo(0, p).wait_recv()
            halo(1, p).wait_recv()
        c = cut(p)
        k = jnp.concatenate([kw[:, c], kprev[:, c]], 0)
        vv = jnp.concatenate([v[:, c], vprev[:, c]], 0)
        qs, gs = both_halves(qw[:, c], 0.125), both_halves(g[:, c])
        hidden = bias[...]
        s = dot(qs, k, 1, 1) + jnp.concatenate([hidden, hidden], 0)
        m = jnp.max(s, 1, keepdims=True)
        e = jnp.exp(s - m)
        total = jnp.sum(e, 1, keepdims=True)
        a = e * (1.0 / total)
        low = a.astype(BF)
        res = dot(low, vv, 1, 0)
        inner = jnp.sum(gs.astype(F32) * res, 1, keepdims=True)
        ds = (a * (dot(gs, vv, 1, 1) - inner)).astype(BF)
        win[:, c] = pick(res)
        gqw[:, c] = (pick(dot(ds, k, 1, 0)) * 0.125).astype(BF)
        dwk[:, c] = dot(ds[:, :tok], qs, 0, 0)
        dwv[:, c] = dot(low[:, :tok], gs, 0, 0)
        logsum = m + jnp.log(total)
        old = stat[...]
        for hh in range(2):
            part = slice(hh * tok, (hh + 1) * tok)
            old = jnp.where(lanes2 == 2 * p + hh, logsum[part], old)
            old = jnp.where(lanes2 == heads + 2 * p + hh, inner[part], old)
        stat[...] = old

    def f_step(p):
        @pl.when(jnp.logical_not(first))
        def _():
            f_copy(p).wait_recv()

        @pl.when(jnp.logical_not(last))
        def _():
            f_out[p] = (f_in[p].astype(F32) + s_own[p]).astype(BF)
            f_copy(p).start()

    def b_step(p):
        @pl.when(jnp.logical_not(last))
        def _():
            b_copy(p).wait_recv()

        @pl.when(jnp.logical_not(first))
        def _():
            b_out[p] = (b_in[p].astype(F32) + sb_own[p]).astype(BF)
            b_copy(p).start()

    def phase_d(p):
        c = cut(p)
        vv, r, pre = v[:, c], rden[p], f_in[p]
        num = dot(kern[p], vv, 1, 0)
        num = jnp.where(lane < DH, num[:tok] + dot(qf[p, :NF], pre, 0, 0),
                        num[tok:] + dot(qf[p, NF:], pre, 0, 0))
        out = num * r
        mixed[:, c] = (out + win[:, c]).astype(BF)
        prod = g[:, c].astype(F32) * out * r
        zero = jnp.zeros_like(prod)
        dd = -jnp.sum(jnp.concatenate(
            [jnp.where(lane < DH, prod, zero), jnp.where(lane < DH, zero, prod)], 0), 1, keepdims=True)
        one_head = [jnp.where(lanes2 == 2 * p + hh, dd[hh * tok : (hh + 1) * tok], 0.0) for hh in range(2)]
        dden[...] += one_head[0] + one_head[1]
        dm = both_halves(dn[:, c])
        ds = (dot(dm, vv, 1, 1) + dd) * plus[p]
        ds = ds.astype(BF)
        d_feat = dot(jnp.concatenate([pre, ncol[...]], 1),
                     jnp.concatenate([dm, jnp.concatenate(one_head, 0).astype(BF)], 1), 1, 1)
        x = qt[prow(p), :]
        dq = dot(kt[prow(p), :].astype(BF), ds, 1, 1) * 0.25
        dqt[prow(p), :] = jnp.concatenate(
            [dq[:FD, :tok] + pull(x[:FD], d_feat[:, :tok], True),
             dq[FD:, tok:] + pull(x[FD:], d_feat[:, tok:], True)], 0)
        dkt[prow(p), :] += dot(spread_q(p), ds, 1, 0)

    def key_side(p):
        @pl.when(jnp.logical_not(last))
        def _():
            halo(2, p).wait_recv()
            halo(3, p).wait_recv()
        c = cut(p)
        q, gg = qnext[:, c], gnext[:, c]
        q = q * jnp.asarray(0.125, BF)
        s = dot(both_halves(kw[:, c]), q, 1, 1)
        da = dot(both_halves(v[:, c]), gg, 1, 1)
        aa, dd = [], []
        for hh in range(2):
            part = slice(hh * tok, (hh + 1) * tok)
            h = 2 * p + hh
            a = jnp.exp(s[part] - stat_in[pl.ds(h, 1), :] + later[...])
            aa.append(a.astype(BF))
            dd.append((a * (da[part] - stat_in[pl.ds(heads + h, 1), :])).astype(BF))
        dk = dot(jnp.concatenate(dd, 1), both_halves(q), 1, 0)
        gkw[:, c] = (dwk[:, c] + dk).astype(BF)
        dwv[:, c] += dot(jnp.concatenate(aa, 1), both_halves(gg), 1, 0)

    def phase_e(p):
        c = cut(p)
        vv, post = v[:, c], b_in[p]
        dv = dot(kern[p], both_halves(dn[:, c]), 0, 0) + dot(kf[p], both_halves(post), 0, 0)
        dwv[:, c] += dv
        pull_keys(p, dot(post, both_halves(vv), 1, 1))

    def pull_keys(p, d_feat):
        x = kt[prow(p), :]
        dkt[prow(p), :] += jnp.concatenate(
            [pull(x[:FD], d_feat[:, :tok], False), pull(x[FD:], d_feat[:, tok:], False)], 0)

    def back_norm(h):
        one = jnp.broadcast_to(dden[pl.ds(h, 1), :], (8, tok)).astype(BF)
        feats = qf[h // 2, pl.ds(pl.multiple_of(lax.rem(h, 2) * NF, 16), NF), :]
        nbown[pl.ds(h, 1), 0:NF] = dot(one, feats, 1, 1)[0:1]

    def finish(p):
        c = cut(p)
        gv[:, c] = dwv[:, c].astype(BF)
        one_head = [jnp.where(lanes2 == 2 * p + hh, 1.0, 0.0).astype(BF) for hh in range(2)]
        pull_keys(p, dot(nbcol[...], jnp.concatenate(one_head, 0), 1, 1))

    hop = 2
    turns = max(hop * (n - 1), pairs) + pairs
    key_at = max(pairs + 2, turns - 6)
    d_at = jnp.maximum(pairs, hop * me)
    e_at = jnp.maximum(pairs, hop * (n - 1 - me))

    def within(p, body):
        @pl.when(jnp.logical_and(p >= 0, p < pairs))
        def _():
            body(p)

    def wave(j):
        within(j - hop * me, f_step)
        within(j - hop * (n - 1 - me), b_step)

        @pl.when(j < pairs)
        def _():
            send_back(j)
            window(j)

        @pl.when(j == pairs - 1)
        def _():
            stat_t[...] = stat[...].T[0 : 2 * heads]

            @pl.when(jnp.logical_not(first))
            def _():
                stats_copy().start()

        within(j - d_at, phase_d)

        @pl.when(j == d_at + pairs - 1)
        def _():
            dden[...] = dden[...].T
            loop(0, heads, back_norm)
            loop(0, me, lambda i: nb_copy(i).start())

        within(j - e_at, phase_e)

        @pl.when(jnp.logical_and(j == key_at, jnp.logical_not(last)))
        def _():
            stats_copy().wait_recv()

        within(j - key_at, key_side)

    loop(0, turns, wave)
    loop(min(turns - key_at, pairs), pairs, key_side)
    gql[...] = dqt[...].T.astype(BF)
    nbcol[...] = gathered(me + 1, n, nb_from, nball)
    loop(0, pairs, finish)
    gkl[...] = dkt[...].T.astype(BF)

    def drain(p):
        @pl.when(jnp.logical_not(last))
        def _():
            halo(0, p).wait_send()
            halo(1, p).wait_send()
            f_copy(p).wait_send()

        @pl.when(jnp.logical_not(first))
        def _():
            halo(2, p).wait_send()
            halo(3, p).wait_send()
            b_copy(p).wait_send()

    loop(0, pairs, drain)
    loop(me + 1, n, lambda j: n_copy(j).wait_send())
    loop(0, me, lambda j: nb_copy(j).wait_send())

    @pl.when(jnp.logical_not(first))
    def _():
        stats_copy().wait_send()


def writer(*refs):
    count = 6
    held, load_s, store_s = refs[2 * count : 3 * count], refs[-2], refs[-1]
    loads = [pltpu.make_async_copy(refs[i], held[i], load_s.at[i]) for i in range(count)]
    stores = [pltpu.make_async_copy(held[i], refs[count + i], store_s.at[i]) for i in range(count)]
    for c in loads:
        c.start()
    for c, d in zip(loads, stores):
        c.wait()
        d.start()
    for d in stores:
        d.wait()


def local(n, axis, *args):
    ql, v = args[0], args[4]
    tok, width = v.shape
    lin = ql.shape[1]
    pairs = width // 128
    heads = 2 * pairs
    vm = pltpu.VMEM
    dma = pltpu.SemaphoreType.DMA
    state16 = vm((pairs, NF, 128), BF)
    state32 = vm((pairs, NF, 128), F32)
    rows = vm((heads, 256), F32)
    wide32 = vm((tok, width), F32)
    wide16 = vm((tok, width), BF)
    lin16 = vm((tok, lin), BF)
    lin32 = vm((lin, tok), F32)
    tile32 = vm((pairs, tok, 128), F32)
    feats = vm((pairs, 2 * NF, tok), BF)
    small = vm((tok, 128), F32)
    scratch = [
        lin16, lin16, wide16, wide16, wide16, wide16,
        vm((tok, 2 * tok), F32), vm((tok, tok), F32), vm((tok, tok), F32),
        lin32, lin32, feats, feats, vm((pairs, 2 * tok, tok), BF), vm((pairs, 2 * tok, tok), F32), tile32,
        rows, vm((n, heads, 256), F32), vm((NF, 128), BF), state32, state16, state16,
        state32, state16, state16, tile32, wide16, wide32, wide32, wide32,
        small, small, vm((2 * heads, tok), F32), vm((2 * heads, tok), F32),
        rows, vm((n, heads, 256), F32), vm((NF, 128), BF),
        wide16, wide16, wide16, wide16, lin32, lin32,
        dma((6,)), dma((4, pairs)), dma((4, pairs)), dma((n,)), dma((n,)), dma((n,)), dma((n,)),
        dma((pairs,)), dma((pairs,)), dma((pairs,)), dma((pairs,)), dma, dma,
    ]
    order = (v, ql, ql, v, v, v)
    shapes = tuple(jax.ShapeDtypeStruct(a.shape, BF) for a in order)
    hbm = pl.BlockSpec(memory_space=pltpu.HBM)
    anywhere = pl.BlockSpec(memory_space=pl.ANY)
    made = pl.pallas_call(
        functools.partial(kernel, n, axis),
        out_shape=shapes,
        in_specs=[hbm] * 6,
        out_specs=tuple([pl.BlockSpec(memory_space=pltpu.VMEM)] * 6),
        scratch_shapes=scratch,
        compiler_params=pltpu.CompilerParams(
            collective_id=0, has_side_effects=True, vmem_limit_bytes=60 * 1024 * 1024),
    )(*args)
    return pl.pallas_call(
        writer,
        out_shape=shapes,
        in_specs=[anywhere] * 6,
        out_specs=tuple([anywhere] * 6),
        scratch_shapes=[vm(a.shape, BF) for a in order] + [dma((6,)), dma((6,))],
        compiler_params=pltpu.CompilerParams(vmem_limit_bytes=60 * 1024 * 1024),
    )(*made)


def solution(mesh):
    place = P(("dp", "seq"), None)
    return jax.shard_map(
        functools.partial(local, mesh.shape["seq"], "seq"),
        mesh=mesh,
        in_specs=(place,) * 6,
        out_specs=(place,) * 6,
        check_vma=False,
    )
```

```python
import functools

import jax
import jax.numpy as jnp
from jax import lax
from jax.experimental import pallas as pl
from jax.experimental.pallas import tpu as pltpu
from jax.sharding import PartitionSpec as P

FD = 16
DH = 64
NF = 160
F32 = jnp.float32
BF = jnp.bfloat16


def dot(a, b, ca, cb):
    return lax.dot_general(a, b, (((ca,), (cb,)), ((), ())), preferred_element_type=F32)


def turned(x, d):
    return x if d == 0 else jnp.concatenate([x[d:], x[:d]], 0)


def features(x, query):
    pair = 1.0 / 16.0 if query else 1.0
    parts = [x * x * (pair * 0.5 if query else 1.0)]
    scaled = x * pair
    for d in range(1, 8):
        parts.append(scaled * turned(x, d))
    parts.append(scaled[:8] * x[8:])
    parts.append(x * 0.25 if query else x)
    row = lax.broadcasted_iota(jnp.int32, (8, x.shape[1]), 0)
    parts.append(jnp.where(row == 0, 1.0, 0.0).astype(F32))
    return jnp.concatenate(parts, 0)


def pull(x, d_feat, query):
    pair = 1.0 / 16.0 if query else 1.0
    total = d_feat[0:16] * x * (pair if query else 2.0)
    cross = jnp.zeros_like(x)
    for d in range(1, 8):
        part = d_feat[16 * d : 16 * d + 16]
        cross = cross + part * turned(x, d) + turned(part * x, 16 - d)
    last = d_feat[128:136]
    cross = cross + jnp.concatenate([last * x[8:], last * x[:8]], 0)
    line = d_feat[136:152]
    return total + cross * pair + line * (0.25 if query else 1.0)


def kernel(n, axis, ql_h, kl_h, qw_h, kw_h, v_h, g_h, mixed, gql, gkl, gqw, gkw, gv,
           ql, kl, qw, kw, v, g,
           bias, later, tri, qt, kt, qf, kf, kern, plus, ksum, nown, nall, ncol, s_own, f_in, f_out,
           sb_own, b_in, b_out, rden, dn, win, dwk, dwv, dden, stat, stat_t, stat_in,
           nbown, nball, nbcol, kprev, vprev, qnext, gnext, dqt, dkt,
           in_s, halo_s, halo_r, n_s, n_r, nb_s, nb_r, f_s, f_r, b_s, b_r, st_s, st_r):
    me = lax.axis_index(axis)
    tok = ql.shape[0]
    pairs = v.shape[1] // 128
    heads = 2 * pairs
    first, last = me == 0, me == n - 1
    lane = lax.broadcasted_iota(jnp.int32, (1, 128), 1)
    half = [(lane < DH).astype(F32).astype(BF), (lane >= DH).astype(F32).astype(BF)]
    rows = lax.broadcasted_iota(jnp.int32, (tok, tok), 0)
    cols = lax.broadcasted_iota(jnp.int32, (tok, tok), 1)
    lanes2 = lax.broadcasted_iota(jnp.int32, (tok, 128), 1)
    causal = cols <= rows

    def cut(p):
        return pl.ds(pl.multiple_of(p * 128, 128), 128)

    def prow(p):
        return pl.ds(pl.multiple_of(p * 2 * FD, 2 * FD), 2 * FD)

    def both_halves(x, scale=None):
        if scale is not None:
            x = x * jnp.asarray(scale, BF)
        return jnp.concatenate([x * half[0], x * half[1]], 0)

    def pick(x):
        m = x.shape[0] // 2
        return jnp.where(lane < DH, x[:m], x[m:])

    def remote(src, dst, ss, rs, to):
        return pltpu.make_async_remote_copy(
            src_ref=src, dst_ref=dst, send_sem=ss, recv_sem=rs,
            device_id={axis: to}, device_id_type=pl.DeviceIdType.MESH)

    def halo(which, p):
        src = (kw_h, v_h, qw_h, g_h)[which]
        dst = (kprev, vprev, qnext, gnext)[which]
        to = me + 1 if which < 2 else me - 1
        return remote(src.at[:, cut(p)], dst.at[:, cut(p)],
                      halo_s.at[which, p], halo_r.at[which, p], to)

    def f_copy(p):
        return remote(f_out.at[p], f_in.at[p], f_s.at[p], f_r.at[p], me + 1)

    def b_copy(p):
        return remote(b_out.at[p], b_in.at[p], b_s.at[p], b_r.at[p], me - 1)

    def n_copy(to):
        return remote(nown, nall.at[me], n_s.at[to], n_r.at[me], to)

    def nb_copy(to):
        return remote(nbown, nball.at[me], nb_s.at[to], nb_r.at[me], to)

    def n_from(j):
        return remote(nown, nall.at[j], n_s.at[j], n_r.at[j], j)

    def nb_from(j):
        return remote(nbown, nball.at[j], nb_s.at[j], nb_r.at[j], j)

    def stats_copy():
        return remote(stat_t, stat_in, st_s, st_r, me - 1)

    def loop(low, high, body):
        def one(i, c):
            body(i)
            return c
        lax.fori_loop(low, high, one, 0)

    barrier = pltpu.get_barrier_semaphore()
    for d in range(1, n):
        pl.semaphore_signal(barrier, inc=1, device_id={axis: lax.rem(me + d, n)},
                            device_id_type=pl.DeviceIdType.MESH)

    fetch = [pltpu.make_async_copy(a, b, in_s.at[i]) for i, (a, b) in enumerate(
        ((kl_h, kl), (v_h, v), (ql_h, ql), (g_h, g), (kw_h, kw), (qw_h, qw)))]
    for f in fetch:
        f.start()
    nown[...] = jnp.zeros_like(nown)
    nbown[...] = jnp.zeros_like(nbown)
    dden[...] = jnp.zeros_like(dden)
    stat[...] = jnp.zeros_like(stat)
    ones8 = jnp.ones((8, tok), BF)
    ones = jnp.ones((128, 128), BF)
    ones2 = jnp.ones((2 * tok, 128), BF)
    never = jnp.full((tok, tok), -1e30, F32)
    none = jnp.zeros((tok, tok), F32)
    tri[...] = jnp.where(causal, 1.0, 0.0)
    bias[:, :tok] = jnp.where(causal, none, never)
    bias[:, tok:] = jnp.where(jnp.logical_and(cols > rows, me > 0), none, never)
    later[...] = jnp.where(jnp.logical_and(rows > cols, me < n - 1), none, never)
    dkt[...] = jnp.zeros_like(dkt)

    @pl.when(first)
    def _():
        kprev[...] = jnp.zeros_like(kprev)
        vprev[...] = jnp.zeros_like(vprev)
        f_in[...] = jnp.zeros_like(f_in)

    @pl.when(last)
    def _():
        qnext[...] = jnp.zeros_like(qnext)
        gnext[...] = jnp.zeros_like(gnext)
        stat_in[...] = jnp.zeros_like(stat_in)
        b_in[...] = jnp.zeros_like(b_in)

    fetch[0].wait()
    kt[...] = kl[...].astype(F32).T
    fetch[1].wait()

    def pair_features(x, query):
        return jnp.concatenate([features(x[:FD], query), features(x[FD:], query)], 0).astype(BF)

    def phase_a(p):
        feats = pair_features(kt[prow(p), :], False)
        kf[p] = feats
        nown[pl.ds(2 * p, 1), 0:NF] = dot(ones8, feats[:NF], 1, 1)[0:1]
        nown[pl.ds(2 * p + 1, 1), 0:NF] = dot(ones8, feats[NF:], 1, 1)[0:1]
        s_own[p] = pick(dot(feats, v[:, cut(p)], 1, 0))

    loop(0, pairs, phase_a)
    pl.semaphore_wait(barrier, n - 1)
    loop(me + 1, n, lambda j: n_copy(j).start())

    def send_front(p):
        @pl.when(jnp.logical_not(last))
        def _():
            halo(0, p).start()
            halo(1, p).start()

    def send_back(p):
        @pl.when(jnp.logical_not(first))
        def _():
            halo(2, p).start()
            halo(3, p).start()

    fetch[2].wait()
    qt[...] = ql[...].astype(F32).T

    def spread_q(p):
        x = (qt[prow(p), :] * 0.25).astype(BF)
        z = jnp.zeros((FD, tok), BF)
        return jnp.concatenate(
            [jnp.concatenate([x[:FD], z], 0), jnp.concatenate([z, x[FD:]], 0)], 1)

    def phase_b(p):
        send_front(p)
        qf[p] = pair_features(qt[prow(p), :], True)
        s = dot(spread_q(p), kt[prow(p), :].astype(BF), 0, 0)
        mask = jnp.concatenate([tri[...], tri[...]], 0)
        kk = mask * (1.0 + s + 0.5 * s * s)
        low = kk.astype(BF)
        kern[p] = low
        plus[p] = mask * (1.0 + s)
        ksum[p] = pick(dot(low, ones, 1, 0))

    loop(0, pairs, phase_b)

    def gathered(low, high, arrive, slots):
        def one(j, total):
            arrive(j).wait_recv()
            return total + slots[j]
        total = lax.fori_loop(low, high, one, jnp.zeros(nown.shape, F32))
        full = jnp.concatenate([total, jnp.zeros((128 - heads, nown.shape[1]), F32)], 0)
        return full.T[0:NF].astype(BF)

    ncol[...] = gathered(0, me, n_from, nall)
    fetch[3].wait()

    def phase_c(p):
        prior = []
        for hh in range(2):
            every = dot(qf[p, hh * NF : (hh + 1) * NF], ncol[...], 0, 0)
            prior.append(jnp.sum(jnp.where(lanes2 == 2 * p + hh, every, 0.0), 1, keepdims=True))
        r = 1.0 / (ksum[p] + jnp.where(lane < DH, prior[0], prior[1]))
        rden[p] = r
        low = (g[:, cut(p)].astype(F32) * r).astype(BF)
        dn[:, cut(p)] = low
        sb_own[p] = pick(dot(qf[p], low, 1, 0))

    loop(0, pairs, phase_c)
    fetch[4].wait()
    fetch[5].wait()

    def window(p):
        @pl.when(jnp.logical_not(first))
        def _():
            halo(0, p).wait_recv()
            halo(1, p).wait_recv()
        c = cut(p)
        k = jnp.concatenate([kw[:, c], kprev[:, c]], 0)
        vv = jnp.concatenate([v[:, c], vprev[:, c]], 0)
        qs, gs = both_halves(qw[:, c], 0.125), both_halves(g[:, c])
        hidden = bias[...]
        s = dot(qs, k, 1, 1) + jnp.concatenate([hidden, hidden], 0)
        m = jnp.max(s, 1, keepdims=True)
        e = jnp.exp(s - m)
        res = dot(e.astype(BF), jnp.concatenate([vv, ones2], 1), 1, 0)
        total = res[:, 128:]
        inv = 1.0 / total
        a = e * jnp.concatenate([inv, inv], 1)
        low = a.astype(BF)
        res = res[:, :128] * inv
        inner = dot((gs.astype(F32) * res).astype(BF), ones, 1, 0)
        ds = (a * (dot(gs, vv, 1, 1) - jnp.concatenate([inner, inner], 1))).astype(BF)
        win[:, c] = pick(res)
        gqw[:, c] = (pick(dot(ds, k, 1, 0)) * 0.125).astype(BF)
        dwk[:, c] = dot(ds[:, :tok], qs, 0, 0)
        dwv[:, c] = dot(low[:, :tok], gs, 0, 0)
        logsum = m + jnp.log(total)
        old = stat[...]
        for hh in range(2):
            part = slice(hh * tok, (hh + 1) * tok)
            old = jnp.where(lanes2 == 2 * p + hh, logsum[part], old)
            old = jnp.where(lanes2 == heads + 2 * p + hh, inner[part], old)
        stat[...] = old

    def f_step(p):
        @pl.when(jnp.logical_not(first))
        def _():
            f_copy(p).wait_recv()

        @pl.when(jnp.logical_not(last))
        def _():
            f_out[p] = (f_in[p].astype(F32) + s_own[p]).astype(BF)
            f_copy(p).start()

    def b_step(p):
        @pl.when(jnp.logical_not(last))
        def _():
            b_copy(p).wait_recv()

        @pl.when(jnp.logical_not(first))
        def _():
            b_out[p] = (b_in[p].astype(F32) + sb_own[p]).astype(BF)
            b_copy(p).start()

    def phase_d(p):
        c = cut(p)
        vv, r, pre = v[:, c], rden[p], f_in[p]
        num = dot(kern[p], vv, 1, 0)
        num = jnp.where(lane < DH, num[:tok] + dot(qf[p, :NF], pre, 0, 0),
                        num[tok:] + dot(qf[p, NF:], pre, 0, 0))
        out = num * r
        mixed[:, c] = (out + win[:, c]).astype(BF)
        prod = g[:, c].astype(F32) * out * r
        dd = dot(both_halves(-prod.astype(BF)), ones, 1, 0)
        one_head = [jnp.where(lanes2 == 2 * p + hh, dd[hh * tok : (hh + 1) * tok], 0.0) for hh in range(2)]
        dden[...] += one_head[0] + one_head[1]
        dm = both_halves(dn[:, c])
        ds = (dot(dm, vv, 1, 1) + dd) * plus[p]
        ds = ds.astype(BF)
        d_feat = dot(jnp.concatenate([pre, ncol[...]], 1),
                     jnp.concatenate([dm, jnp.concatenate(one_head, 0).astype(BF)], 1), 1, 1)
        x = qt[prow(p), :]
        dq = dot(kt[prow(p), :].astype(BF), ds, 1, 1) * 0.25
        dqt[prow(p), :] = jnp.concatenate(
            [dq[:FD, :tok] + pull(x[:FD], d_feat[:, :tok], True),
             dq[FD:, tok:] + pull(x[FD:], d_feat[:, tok:], True)], 0)
        dkt[prow(p), :] += dot(spread_q(p), ds, 1, 0)

    def key_side(p):
        @pl.when(jnp.logical_not(last))
        def _():
            halo(2, p).wait_recv()
            halo(3, p).wait_recv()
        c = cut(p)
        q, gg = qnext[:, c], gnext[:, c]
        q = q * jnp.asarray(0.125, BF)
        s = dot(both_halves(kw[:, c]), q, 1, 1)
        da = dot(both_halves(v[:, c]), gg, 1, 1)
        aa, dd = [], []
        for hh in range(2):
            part = slice(hh * tok, (hh + 1) * tok)
            h = 2 * p + hh
            a = jnp.exp(s[part] - stat_in[pl.ds(h, 1), :] + later[...])
            aa.append(a.astype(BF))
            dd.append((a * (da[part] - stat_in[pl.ds(heads + h, 1), :])).astype(BF))
        dk = dot(jnp.concatenate(dd, 1), both_halves(q), 1, 0)
        gkw[:, c] = (dwk[:, c] + dk).astype(BF)
        dwv[:, c] += dot(jnp.concatenate(aa, 1), both_halves(gg), 1, 0)

    def phase_e(p):
        c = cut(p)
        vv, post = v[:, c], b_in[p]
        dv = dot(kern[p], both_halves(dn[:, c]), 0, 0) + dot(kf[p], both_halves(post), 0, 0)
        dwv[:, c] += dv
        pull_keys(p, dot(post, both_halves(vv), 1, 1))

    def pull_keys(p, d_feat):
        x = kt[prow(p), :]
        dkt[prow(p), :] += jnp.concatenate(
            [pull(x[:FD], d_feat[:, :tok], False), pull(x[FD:], d_feat[:, tok:], False)], 0)

    def back_norm(h):
        one = jnp.broadcast_to(dden[pl.ds(h, 1), :], (8, tok)).astype(BF)
        feats = qf[h // 2, pl.ds(pl.multiple_of(lax.rem(h, 2) * NF, 16), NF), :]
        nbown[pl.ds(h, 1), 0:NF] = dot(one, feats, 1, 1)[0:1]

    def finish(p):
        c = cut(p)
        gv[:, c] = dwv[:, c].astype(BF)
        one_head = [jnp.where(lanes2 == 2 * p + hh, 1.0, 0.0).astype(BF) for hh in range(2)]
        pull_keys(p, dot(nbcol[...], jnp.concatenate(one_head, 0), 1, 1))

    hop = 2
    turns = max(hop * (n - 1), pairs) + pairs
    key_at = max(pairs + 2, turns - 6)
    d_at = jnp.maximum(pairs, hop * me)
    e_at = jnp.maximum(pairs, hop * (n - 1 - me))

    def within(p, body):
        @pl.when(jnp.logical_and(p >= 0, p < pairs))
        def _():
            body(p)

    def wave(j):
        within(j - hop * me, f_step)
        within(j - hop * (n - 1 - me), b_step)

        @pl.when(j < pairs)
        def _():
            send_back(j)
            window(j)

        @pl.when(j == pairs - 1)
        def _():
            stat_t[...] = stat[...].T[0 : 2 * heads]

            @pl.when(jnp.logical_not(first))
            def _():
                stats_copy().start()

        within(j - d_at, phase_d)

        @pl.when(j == d_at + pairs - 1)
        def _():
            dden[...] = dden[...].T
            loop(0, heads, back_norm)
            loop(0, me, lambda i: nb_copy(i).start())

        within(j - e_at, phase_e)

        @pl.when(jnp.logical_and(j == key_at, jnp.logical_not(last)))
        def _():
            stats_copy().wait_recv()

        within(j - key_at, key_side)

    loop(0, turns, wave)
    loop(min(turns - key_at, pairs), pairs, key_side)
    gql[...] = dqt[...].T.astype(BF)
    nbcol[...] = gathered(me + 1, n, nb_from, nball)
    loop(0, pairs, finish)
    gkl[...] = dkt[...].T.astype(BF)

    def drain(p):
        @pl.when(jnp.logical_not(last))
        def _():
            halo(0, p).wait_send()
            halo(1, p).wait_send()
            f_copy(p).wait_send()

        @pl.when(jnp.logical_not(first))
        def _():
            halo(2, p).wait_send()
            halo(3, p).wait_send()
            b_copy(p).wait_send()

    loop(0, pairs, drain)
    loop(me + 1, n, lambda j: n_copy(j).wait_send())
    loop(0, me, lambda j: nb_copy(j).wait_send())

    @pl.when(jnp.logical_not(first))
    def _():
        stats_copy().wait_send()


def writer(*refs):
    count = 6
    held, load_s, store_s = refs[2 * count : 3 * count], refs[-2], refs[-1]
    loads = [pltpu.make_async_copy(refs[i], held[i], load_s.at[i]) for i in range(count)]
    stores = [pltpu.make_async_copy(held[i], refs[count + i], store_s.at[i]) for i in range(count)]
    for c in loads:
        c.start()
    for c, d in zip(loads, stores):
        c.wait()
        d.start()
    for d in stores:
        d.wait()


def local(n, axis, *args):
    ql, v = args[0], args[4]
    tok, width = v.shape
    lin = ql.shape[1]
    pairs = width // 128
    heads = 2 * pairs
    vm = pltpu.VMEM
    dma = pltpu.SemaphoreType.DMA
    state16 = vm((pairs, NF, 128), BF)
    state32 = vm((pairs, NF, 128), F32)
    rows = vm((heads, 256), F32)
    wide32 = vm((tok, width), F32)
    wide16 = vm((tok, width), BF)
    lin16 = vm((tok, lin), BF)
    lin32 = vm((lin, tok), F32)
    tile32 = vm((pairs, tok, 128), F32)
    feats = vm((pairs, 2 * NF, tok), BF)
    small = vm((tok, 128), F32)
    scratch = [
        lin16, lin16, wide16, wide16, wide16, wide16,
        vm((tok, 2 * tok), F32), vm((tok, tok), F32), vm((tok, tok), F32),
        lin32, lin32, feats, feats, vm((pairs, 2 * tok, tok), BF), vm((pairs, 2 * tok, tok), F32), tile32,
        rows, vm((n, heads, 256), F32), vm((NF, 128), BF), state32, state16, state16,
        state32, state16, state16, tile32, wide16, wide32, wide32, wide32,
        small, small, vm((2 * heads, tok), F32), vm((2 * heads, tok), F32),
        rows, vm((n, heads, 256), F32), vm((NF, 128), BF),
        wide16, wide16, wide16, wide16, lin32, lin32,
        dma((6,)), dma((4, pairs)), dma((4, pairs)), dma((n,)), dma((n,)), dma((n,)), dma((n,)),
        dma((pairs,)), dma((pairs,)), dma((pairs,)), dma((pairs,)), dma, dma,
    ]
    order = (v, ql, ql, v, v, v)
    shapes = tuple(jax.ShapeDtypeStruct(a.shape, BF) for a in order)
    hbm = pl.BlockSpec(memory_space=pltpu.HBM)
    anywhere = pl.BlockSpec(memory_space=pl.ANY)
    made = pl.pallas_call(
        functools.partial(kernel, n, axis),
        out_shape=shapes,
        in_specs=[hbm] * 6,
        out_specs=tuple([pl.BlockSpec(memory_space=pltpu.VMEM)] * 6),
        scratch_shapes=scratch,
        compiler_params=pltpu.CompilerParams(
            collective_id=0, has_side_effects=True, vmem_limit_bytes=60 * 1024 * 1024),
    )(*args)
    return pl.pallas_call(
        writer,
        out_shape=shapes,
        in_specs=[anywhere] * 6,
        out_specs=tuple([anywhere] * 6),
        scratch_shapes=[vm(a.shape, BF) for a in order] + [dma((6,)), dma((6,))],
        compiler_params=pltpu.CompilerParams(vmem_limit_bytes=60 * 1024 * 1024),
    )(*made)


def solution(mesh):
    place = P(("dp", "seq"), None)
    return jax.shard_map(
        functools.partial(local, mesh.shape["seq"], "seq"),
        mesh=mesh,
        in_specs=(place,) * 6,
        out_specs=(place,) * 6,
        check_vma=False,
    )
```

```python
import functools

import jax
import jax.numpy as jnp
from jax import lax
from jax.experimental import pallas as pl
from jax.experimental.pallas import tpu as pltpu
from jax.sharding import PartitionSpec as P

FD = 16
DH = 64
NF = 160
F32 = jnp.float32
BF = jnp.bfloat16


def dot(a, b, ca, cb):
    return lax.dot_general(a, b, (((ca,), (cb,)), ((), ())), preferred_element_type=F32)


def turned(x, d):
    return x if d == 0 else jnp.concatenate([x[d:], x[:d]], 0)


def features(x, query):
    pair = 1.0 / 16.0 if query else 1.0
    parts = [x * x * (pair * 0.5 if query else 1.0)]
    scaled = x * pair
    for d in range(1, 8):
        parts.append(scaled * turned(x, d))
    parts.append(scaled[:8] * x[8:])
    parts.append(x * 0.25 if query else x)
    row = lax.broadcasted_iota(jnp.int32, (8, x.shape[1]), 0)
    parts.append(jnp.where(row == 0, 1.0, 0.0).astype(F32))
    return jnp.concatenate(parts, 0)


def pull(x, d_feat, query):
    pair = 1.0 / 16.0 if query else 1.0
    total = d_feat[0:16] * x * (pair if query else 2.0)
    cross = jnp.zeros_like(x)
    for d in range(1, 8):
        part = d_feat[16 * d : 16 * d + 16]
        cross = cross + part * turned(x, d) + turned(part * x, 16 - d)
    last = d_feat[128:136]
    cross = cross + jnp.concatenate([last * x[8:], last * x[:8]], 0)
    line = d_feat[136:152]
    return total + cross * pair + line * (0.25 if query else 1.0)


def kernel(n, axis, ql_h, kl_h, qw_h, kw_h, v_h, g_h, mixed, gql, gkl, gqw, gkw, gv,
           ql, kl, qw, kw, v, g,
           bias, later, tri, qt, kt, qf, kf, kern, plus, ksum, nown, nall, ncol, s_own, f_in, f_out,
           sb_own, b_in, b_out, rden, dn, win, dwk, dwv, dden, stat, stat_t, stat_in,
           nbown, nball, nbcol, kprev, vprev, qnext, gnext, dqt, dkt,
           in_s, halo_s, halo_r, n_s, n_r, nb_s, nb_r, f_s, f_r, b_s, b_r, st_s, st_r):
    me = lax.axis_index(axis)
    tok = ql.shape[0]
    pairs = v.shape[1] // 128
    heads = 2 * pairs
    first, last = me == 0, me == n - 1
    lane = lax.broadcasted_iota(jnp.int32, (1, 128), 1)
    half = [(lane < DH).astype(F32).astype(BF), (lane >= DH).astype(F32).astype(BF)]
    rows = lax.broadcasted_iota(jnp.int32, (tok, tok), 0)
    cols = lax.broadcasted_iota(jnp.int32, (tok, tok), 1)
    lanes2 = lax.broadcasted_iota(jnp.int32, (tok, 128), 1)
    causal = cols <= rows

    def cut(p):
        return pl.ds(pl.multiple_of(p * 128, 128), 128)

    def prow(p):
        return pl.ds(pl.multiple_of(p * 2 * FD, 2 * FD), 2 * FD)

    def both_halves(x, scale=None):
        if scale is not None:
            x = x * jnp.asarray(scale, BF)
        return jnp.concatenate([x * half[0], x * half[1]], 0)

    def pick(x):
        m = x.shape[0] // 2
        return jnp.where(lane < DH, x[:m], x[m:])

    def remote(src, dst, ss, rs, to):
        return pltpu.make_async_remote_copy(
            src_ref=src, dst_ref=dst, send_sem=ss, recv_sem=rs,
            device_id={axis: to}, device_id_type=pl.DeviceIdType.MESH)

    step = tok // pairs

    def halo(which, p):
        src = (kw_h, v_h, qw_h, g_h)[which]
        dst = (kprev, vprev, qnext, gnext)[which]
        to = me + 1 if which < 2 else me - 1
        part = pl.ds(pl.multiple_of(p * step, step), step)
        return remote(src.at[part, :], dst.at[part, :],
                      halo_s.at[which, p], halo_r.at[which, p], to)

    def f_copy(p):
        return remote(f_out.at[p], f_in.at[p], f_s.at[p], f_r.at[p], me + 1)

    def b_copy(p):
        return remote(b_out.at[p], b_in.at[p], b_s.at[p], b_r.at[p], me - 1)

    def n_copy(to):
        return remote(nown, nall.at[me], n_s.at[to], n_r.at[me], to)

    def nb_copy(to):
        return remote(nbown, nball.at[me], nb_s.at[to], nb_r.at[me], to)

    def n_from(j):
        return remote(nown, nall.at[j], n_s.at[j], n_r.at[j], j)

    def nb_from(j):
        return remote(nbown, nball.at[j], nb_s.at[j], nb_r.at[j], j)

    def stats_copy():
        return remote(stat_t, stat_in, st_s, st_r, me - 1)

    def loop(low, high, body):
        def one(i, c):
            body(i)
            return c
        lax.fori_loop(low, high, one, 0)

    barrier = pltpu.get_barrier_semaphore()
    for d in range(1, n):
        pl.semaphore_signal(barrier, inc=1, device_id={axis: lax.rem(me + d, n)},
                            device_id_type=pl.DeviceIdType.MESH)

    fetch = [pltpu.make_async_copy(a, b, in_s.at[i]) for i, (a, b) in enumerate(
        ((kl_h, kl), (v_h, v), (ql_h, ql), (g_h, g), (kw_h, kw), (qw_h, qw)))]
    for f in fetch:
        f.start()
    nown[...] = jnp.zeros_like(nown)
    nbown[...] = jnp.zeros_like(nbown)
    dden[...] = jnp.zeros_like(dden)
    stat[...] = jnp.zeros_like(stat)
    ones8 = jnp.ones((8, tok), BF)
    ones = jnp.ones((128, 128), BF)
    ones2 = jnp.ones((2 * tok, 128), BF)
    never = jnp.full((tok, tok), -1e30, F32)
    none = jnp.zeros((tok, tok), F32)
    tri[...] = jnp.where(causal, 1.0, 0.0)
    bias[:, :tok] = jnp.where(causal, none, never)
    bias[:, tok:] = jnp.where(jnp.logical_and(cols > rows, me > 0), none, never)
    later[...] = jnp.where(jnp.logical_and(rows > cols, me < n - 1), none, never)
    dkt[...] = jnp.zeros_like(dkt)

    @pl.when(first)
    def _():
        kprev[...] = jnp.zeros_like(kprev)
        vprev[...] = jnp.zeros_like(vprev)
        f_in[...] = jnp.zeros_like(f_in)

    @pl.when(last)
    def _():
        qnext[...] = jnp.zeros_like(qnext)
        gnext[...] = jnp.zeros_like(gnext)
        stat_in[...] = jnp.zeros_like(stat_in)
        b_in[...] = jnp.zeros_like(b_in)

    fetch[0].wait()
    kt[...] = kl[...].astype(F32).T
    fetch[1].wait()

    def pair_features(x, query):
        return jnp.concatenate([features(x[:FD], query), features(x[FD:], query)], 0).astype(BF)

    def phase_a(p):
        feats = pair_features(kt[prow(p), :], False)
        kf[p] = feats
        nown[pl.ds(2 * p, 1), 0:NF] = dot(ones8, feats[:NF], 1, 1)[0:1]
        nown[pl.ds(2 * p + 1, 1), 0:NF] = dot(ones8, feats[NF:], 1, 1)[0:1]
        s_own[p] = pick(dot(feats, v[:, cut(p)], 1, 0))

    loop(0, pairs, phase_a)
    pl.semaphore_wait(barrier, n - 1)
    loop(me + 1, n, lambda j: n_copy(j).start())

    def send_front(p):
        @pl.when(jnp.logical_not(last))
        def _():
            halo(0, p).start()
            halo(1, p).start()

    def send_back(p):
        @pl.when(jnp.logical_not(first))
        def _():
            halo(2, p).start()
            halo(3, p).start()

    fetch[2].wait()
    qt[...] = ql[...].astype(F32).T

    def spread_q(p):
        x = (qt[prow(p), :] * 0.25).astype(BF)
        z = jnp.zeros((FD, tok), BF)
        return jnp.concatenate(
            [jnp.concatenate([x[:FD], z], 0), jnp.concatenate([z, x[FD:]], 0)], 1)

    def phase_b(p):
        send_front(p)
        qf[p] = pair_features(qt[prow(p), :], True)
        s = dot(spread_q(p), kt[prow(p), :].astype(BF), 0, 0)
        mask = jnp.concatenate([tri[...], tri[...]], 0)
        kk = mask * (1.0 + s + 0.5 * s * s)
        low = kk.astype(BF)
        kern[p] = low
        plus[p] = mask * (1.0 + s)
        ksum[p] = pick(dot(low, ones, 1, 0))

    loop(0, pairs, phase_b)

    def gathered(low, high, arrive, slots):
        def one(j, total):
            arrive(j).wait_recv()
            return total + slots[j]
        total = lax.fori_loop(low, high, one, jnp.zeros(nown.shape, F32))
        full = jnp.concatenate([total, jnp.zeros((128 - heads, nown.shape[1]), F32)], 0)
        return full.T[0:NF].astype(BF)

    ncol[...] = gathered(0, me, n_from, nall)
    fetch[3].wait()

    def phase_c(p):
        prior = []
        for hh in range(2):
            every = dot(qf[p, hh * NF : (hh + 1) * NF], ncol[...], 0, 0)
            prior.append(jnp.sum(jnp.where(lanes2 == 2 * p + hh, every, 0.0), 1, keepdims=True))
        r = 1.0 / (ksum[p] + jnp.where(lane < DH, prior[0], prior[1]))
        rden[p] = r
        low = (g[:, cut(p)].astype(F32) * r).astype(BF)
        dn[:, cut(p)] = low
        sb_own[p] = pick(dot(qf[p], low, 1, 0))

    loop(0, pairs, phase_c)
    fetch[4].wait()
    fetch[5].wait()

    def window(p):
        c = cut(p)
        k = jnp.concatenate([kw[:, c], kprev[:, c]], 0)
        vv = jnp.concatenate([v[:, c], vprev[:, c]], 0)
        qs, gs = both_halves(qw[:, c], 0.125), both_halves(g[:, c])
        hidden = bias[...]
        s = dot(qs, k, 1, 1) + jnp.concatenate([hidden, hidden], 0)
        m = jnp.max(s, 1, keepdims=True)
        e = jnp.exp(s - m)
        res = dot(e.astype(BF), jnp.concatenate([vv, ones2], 1), 1, 0)
        total = res[:, 128:]
        inv = 1.0 / total
        a = e * jnp.concatenate([inv, inv], 1)
        low = a.astype(BF)
        res = res[:, :128] * inv
        inner = dot((gs.astype(F32) * res).astype(BF), ones, 1, 0)
        ds = (a * (dot(gs, vv, 1, 1) - jnp.concatenate([inner, inner], 1))).astype(BF)
        win[:, c] = pick(res)
        gqw[:, c] = (pick(dot(ds, k, 1, 0)) * 0.125).astype(BF)
        dwk[:, c] = dot(ds[:, :tok], qs, 0, 0)
        dwv[:, c] = dot(low[:, :tok], gs, 0, 0)
        logsum = m + jnp.log(total)
        old = stat[...]
        for hh in range(2):
            part = slice(hh * tok, (hh + 1) * tok)
            old = jnp.where(lanes2 == 2 * p + hh, logsum[part], old)
            old = jnp.where(lanes2 == heads + 2 * p + hh, inner[part], old)
        stat[...] = old

    def f_step(p):
        @pl.when(jnp.logical_not(first))
        def _():
            f_copy(p).wait_recv()

        @pl.when(jnp.logical_not(last))
        def _():
            f_out[p] = (f_in[p].astype(F32) + s_own[p]).astype(BF)
            f_copy(p).start()

    def b_step(p):
        @pl.when(jnp.logical_not(last))
        def _():
            b_copy(p).wait_recv()

        @pl.when(jnp.logical_not(first))
        def _():
            b_out[p] = (b_in[p].astype(F32) + sb_own[p]).astype(BF)
            b_copy(p).start()

    def phase_d(p):
        c = cut(p)
        vv, r, pre = v[:, c], rden[p], f_in[p]
        num = dot(kern[p], vv, 1, 0)
        num = jnp.where(lane < DH, num[:tok] + dot(qf[p, :NF], pre, 0, 0),
                        num[tok:] + dot(qf[p, NF:], pre, 0, 0))
        out = num * r
        mixed[:, c] = (out + win[:, c]).astype(BF)
        prod = g[:, c].astype(F32) * out * r
        dd = dot(both_halves(-prod.astype(BF)), ones, 1, 0)
        one_head = [jnp.where(lanes2 == 2 * p + hh, dd[hh * tok : (hh + 1) * tok], 0.0) for hh in range(2)]
        dden[...] += one_head[0] + one_head[1]
        dm = both_halves(dn[:, c])
        ds = (dot(dm, vv, 1, 1) + dd) * plus[p]
        ds = ds.astype(BF)
        d_feat = dot(jnp.concatenate([pre, ncol[...]], 1),
                     jnp.concatenate([dm, jnp.concatenate(one_head, 0).astype(BF)], 1), 1, 1)
        x = qt[prow(p), :]
        dq = dot(kt[prow(p), :].astype(BF), ds, 1, 1) * 0.25
        dqt[prow(p), :] = jnp.concatenate(
            [dq[:FD, :tok] + pull(x[:FD], d_feat[:, :tok], True),
             dq[FD:, tok:] + pull(x[FD:], d_feat[:, tok:], True)], 0)
        dkt[prow(p), :] += dot(spread_q(p), ds, 1, 0)

    def key_side(p):
        c = cut(p)
        q, gg = qnext[:, c], gnext[:, c]
        q = q * jnp.asarray(0.125, BF)
        s = dot(both_halves(kw[:, c]), q, 1, 1)
        da = dot(both_halves(v[:, c]), gg, 1, 1)
        aa, dd = [], []
        for hh in range(2):
            part = slice(hh * tok, (hh + 1) * tok)
            h = 2 * p + hh
            a = jnp.exp(s[part] - stat_in[pl.ds(h, 1), :] + later[...])
            aa.append(a.astype(BF))
            dd.append((a * (da[part] - stat_in[pl.ds(heads + h, 1), :])).astype(BF))
        dk = dot(jnp.concatenate(dd, 1), both_halves(q), 1, 0)
        gkw[:, c] = (dwk[:, c] + dk).astype(BF)
        dwv[:, c] += dot(jnp.concatenate(aa, 1), both_halves(gg), 1, 0)

    def phase_e(p):
        c = cut(p)
        vv, post = v[:, c], b_in[p]
        dv = dot(kern[p], both_halves(dn[:, c]), 0, 0) + dot(kf[p], both_halves(post), 0, 0)
        dwv[:, c] += dv
        pull_keys(p, dot(post, both_halves(vv), 1, 1))

    def pull_keys(p, d_feat):
        x = kt[prow(p), :]
        dkt[prow(p), :] += jnp.concatenate(
            [pull(x[:FD], d_feat[:, :tok], False), pull(x[FD:], d_feat[:, tok:], False)], 0)

    def back_norm(h):
        one = jnp.broadcast_to(dden[pl.ds(h, 1), :], (8, tok)).astype(BF)
        feats = qf[h // 2, pl.ds(pl.multiple_of(lax.rem(h, 2) * NF, 16), NF), :]
        nbown[pl.ds(h, 1), 0:NF] = dot(one, feats, 1, 1)[0:1]

    def finish(p):
        c = cut(p)
        gv[:, c] = dwv[:, c].astype(BF)
        one_head = [jnp.where(lanes2 == 2 * p + hh, 1.0, 0.0).astype(BF) for hh in range(2)]
        pull_keys(p, dot(nbcol[...], jnp.concatenate(one_head, 0), 1, 1))

    hop = 2
    turns = max(hop * (n - 1), pairs) + pairs
    key_at = max(pairs + 2, turns - 6)
    d_at = jnp.maximum(pairs, hop * me)
    e_at = jnp.maximum(pairs, hop * (n - 1 - me))

    def within(p, body):
        @pl.when(jnp.logical_and(p >= 0, p < pairs))
        def _():
            body(p)

    def front_here(p):
        halo(0, p).wait_recv()
        halo(1, p).wait_recv()

    def back_here(p):
        halo(2, p).wait_recv()
        halo(3, p).wait_recv()

    def wave(j):
        within(j - hop * me, f_step)
        within(j - hop * (n - 1 - me), b_step)

        @pl.when(jnp.logical_and(j == 0, jnp.logical_not(first)))
        def _():
            loop(0, pairs, front_here)

        @pl.when(j < pairs)
        def _():
            send_back(j)
            window(j)

        @pl.when(j == pairs - 1)
        def _():
            stat_t[...] = stat[...].T[0 : 2 * heads]

            @pl.when(jnp.logical_not(first))
            def _():
                stats_copy().start()

        within(j - d_at, phase_d)

        @pl.when(j == d_at + pairs - 1)
        def _():
            dden[...] = dden[...].T
            loop(0, heads, back_norm)
            loop(0, me, lambda i: nb_copy(i).start())

        within(j - e_at, phase_e)

        @pl.when(jnp.logical_and(j == key_at, jnp.logical_not(last)))
        def _():
            loop(0, pairs, back_here)
            stats_copy().wait_recv()

        within(j - key_at, key_side)

    loop(0, turns, wave)
    loop(min(turns - key_at, pairs), pairs, key_side)
    gql[...] = dqt[...].T.astype(BF)
    nbcol[...] = gathered(me + 1, n, nb_from, nball)
    loop(0, pairs, finish)
    gkl[...] = dkt[...].T.astype(BF)

    def drain(p):
        @pl.when(jnp.logical_not(last))
        def _():
            halo(0, p).wait_send()
            halo(1, p).wait_send()
            f_copy(p).wait_send()

        @pl.when(jnp.logical_not(first))
        def _():
            halo(2, p).wait_send()
            halo(3, p).wait_send()
            b_copy(p).wait_send()

    loop(0, pairs, drain)
    loop(me + 1, n, lambda j: n_copy(j).wait_send())
    loop(0, me, lambda j: nb_copy(j).wait_send())

    @pl.when(jnp.logical_not(first))
    def _():
        stats_copy().wait_send()


def writer(*refs):
    count = 6
    held, load_s, store_s = refs[2 * count : 3 * count], refs[-2], refs[-1]
    loads = [pltpu.make_async_copy(refs[i], held[i], load_s.at[i]) for i in range(count)]
    stores = [pltpu.make_async_copy(held[i], refs[count + i], store_s.at[i]) for i in range(count)]
    for c in loads:
        c.start()
    for c, d in zip(loads, stores):
        c.wait()
        d.start()
    for d in stores:
        d.wait()


def local(n, axis, *args):
    ql, v = args[0], args[4]
    tok, width = v.shape
    lin = ql.shape[1]
    pairs = width // 128
    heads = 2 * pairs
    vm = pltpu.VMEM
    dma = pltpu.SemaphoreType.DMA
    state16 = vm((pairs, NF, 128), BF)
    state32 = vm((pairs, NF, 128), F32)
    rows = vm((heads, 256), F32)
    wide32 = vm((tok, width), F32)
    wide16 = vm((tok, width), BF)
    lin16 = vm((tok, lin), BF)
    lin32 = vm((lin, tok), F32)
    tile32 = vm((pairs, tok, 128), F32)
    feats = vm((pairs, 2 * NF, tok), BF)
    small = vm((tok, 128), F32)
    scratch = [
        lin16, lin16, wide16, wide16, wide16, wide16,
        vm((tok, 2 * tok), F32), vm((tok, tok), F32), vm((tok, tok), F32),
        lin32, lin32, feats, feats, vm((pairs, 2 * tok, tok), BF), vm((pairs, 2 * tok, tok), F32), tile32,
        rows, vm((n, heads, 256), F32), vm((NF, 128), BF), state32, state16, state16,
        state32, state16, state16, tile32, wide16, wide32, wide32, wide32,
        small, small, vm((2 * heads, tok), F32), vm((2 * heads, tok), F32),
        rows, vm((n, heads, 256), F32), vm((NF, 128), BF),
        wide16, wide16, wide16, wide16, lin32, lin32,
        dma((6,)), dma((4, pairs)), dma((4, pairs)), dma((n,)), dma((n,)), dma((n,)), dma((n,)),
        dma((pairs,)), dma((pairs,)), dma((pairs,)), dma((pairs,)), dma, dma,
    ]
    order = (v, ql, ql, v, v, v)
    shapes = tuple(jax.ShapeDtypeStruct(a.shape, BF) for a in order)
    hbm = pl.BlockSpec(memory_space=pltpu.HBM)
    anywhere = pl.BlockSpec(memory_space=pl.ANY)
    made = pl.pallas_call(
        functools.partial(kernel, n, axis),
        out_shape=shapes,
        in_specs=[hbm] * 6,
        out_specs=tuple([pl.BlockSpec(memory_space=pltpu.VMEM)] * 6),
        scratch_shapes=scratch,
        compiler_params=pltpu.CompilerParams(
            collective_id=0, has_side_effects=True, vmem_limit_bytes=60 * 1024 * 1024),
    )(*args)
    return pl.pallas_call(
        writer,
        out_shape=shapes,
        in_specs=[anywhere] * 6,
        out_specs=tuple([anywhere] * 6),
        scratch_shapes=[vm(a.shape, BF) for a in order] + [dma((6,)), dma((6,))],
        compiler_params=pltpu.CompilerParams(vmem_limit_bytes=60 * 1024 * 1024),
    )(*made)


def solution(mesh):
    place = P(("dp", "seq"), None)
    return jax.shard_map(
        functools.partial(local, mesh.shape["seq"], "seq"),
        mesh=mesh,
        in_specs=(place,) * 6,
        out_specs=(place,) * 6,
        check_vma=False,
    )
```

```python
import functools

import jax
import jax.numpy as jnp
from jax import lax
from jax.experimental import pallas as pl
from jax.experimental.pallas import tpu as pltpu
from jax.sharding import PartitionSpec as P

FD = 16
DH = 64
NF = 160
F32 = jnp.float32
BF = jnp.bfloat16


def dot(a, b, ca, cb):
    return lax.dot_general(a, b, (((ca,), (cb,)), ((), ())), preferred_element_type=F32)


def turned(x, d):
    return x if d == 0 else jnp.concatenate([x[d:], x[:d]], 0)


def features(x, query):
    pair = 1.0 / 16.0 if query else 1.0
    parts = [x * x * (pair * 0.5 if query else 1.0)]
    scaled = x * pair
    for d in range(1, 8):
        parts.append(scaled * turned(x, d))
    parts.append(scaled[:8] * x[8:])
    parts.append(x * 0.25 if query else x)
    row = lax.broadcasted_iota(jnp.int32, (8, x.shape[1]), 0)
    parts.append(jnp.where(row == 0, 1.0, 0.0).astype(F32))
    return jnp.concatenate(parts, 0)


def pull(x, d_feat, query):
    pair = 1.0 / 16.0 if query else 1.0
    total = d_feat[0:16] * x * (pair if query else 2.0)
    cross = jnp.zeros_like(x)
    for d in range(1, 8):
        part = d_feat[16 * d : 16 * d + 16]
        cross = cross + part * turned(x, d) + turned(part * x, 16 - d)
    last = d_feat[128:136]
    cross = cross + jnp.concatenate([last * x[8:], last * x[:8]], 0)
    line = d_feat[136:152]
    return total + cross * pair + line * (0.25 if query else 1.0)


def kernel(n, axis, ql_h, kl_h, qw_h, kw_h, v_h, g_h, mixed, gql, gkl, gqw, gkw, gv,
           ql, kl, qw, kw, v, g,
           bias, later, tri, qt, kt, qf, kf, kern, plus, ksum, nown, nall, ncol, s_own, f_in, f_out,
           sb_own, b_in, b_out, rden, dn, win, dwk, dwv, dden, stat, stat_t, stat_in,
           nbown, nball, nbcol, kprev, vprev, qnext, gnext, dqt, dkt,
           in_s, halo_s, halo_r, n_s, n_r, nb_s, nb_r, f_s, f_r, b_s, b_r, st_s, st_r):
    me = lax.axis_index(axis)
    tok = ql.shape[0]
    pairs = v.shape[1] // 128
    heads = 2 * pairs
    first, last = me == 0, me == n - 1
    lane = lax.broadcasted_iota(jnp.int32, (1, 128), 1)
    half = [(lane < DH).astype(F32).astype(BF), (lane >= DH).astype(F32).astype(BF)]
    rows = lax.broadcasted_iota(jnp.int32, (tok, tok), 0)
    cols = lax.broadcasted_iota(jnp.int32, (tok, tok), 1)
    lanes2 = lax.broadcasted_iota(jnp.int32, (tok, 128), 1)
    causal = cols <= rows

    def cut(p):
        return pl.ds(pl.multiple_of(p * 128, 128), 128)

    def prow(p):
        return pl.ds(pl.multiple_of(p * 2 * FD, 2 * FD), 2 * FD)

    def both_halves(x, scale=None):
        if scale is not None:
            x = x * jnp.asarray(scale, BF)
        return jnp.concatenate([x * half[0], x * half[1]], 0)

    def pick(x):
        m = x.shape[0] // 2
        return jnp.where(lane < DH, x[:m], x[m:])

    def remote(src, dst, ss, rs, to):
        return pltpu.make_async_remote_copy(
            src_ref=src, dst_ref=dst, send_sem=ss, recv_sem=rs,
            device_id={axis: to}, device_id_type=pl.DeviceIdType.MESH)

    step = tok // pairs

    def halo(which, p):
        src = (kw_h, v_h, qw_h, g_h)[which]
        dst = (kprev, vprev, qnext, gnext)[which]
        to = me + 1 if which < 2 else me - 1
        part = pl.ds(pl.multiple_of(p * step, step), step)
        return remote(src.at[part, :], dst.at[part, :],
                      halo_s.at[which, p], halo_r.at[which, p], to)

    def f_copy(p):
        return remote(f_out.at[p], f_in.at[p], f_s.at[p], f_r.at[p], me + 1)

    def b_copy(p):
        return remote(b_out.at[p], b_in.at[p], b_s.at[p], b_r.at[p], me - 1)

    def n_copy(to):
        return remote(nown, nall.at[me], n_s.at[to], n_r.at[me], to)

    def nb_copy(to):
        return remote(nbown, nball.at[me], nb_s.at[to], nb_r.at[me], to)

    def n_from(j):
        return remote(nown, nall.at[j], n_s.at[j], n_r.at[j], j)

    def nb_from(j):
        return remote(nbown, nball.at[j], nb_s.at[j], nb_r.at[j], j)

    def stats_copy():
        return remote(stat_t, stat_in, st_s, st_r, me - 1)

    def loop(low, high, body):
        def one(i, c):
            body(i)
            return c
        lax.fori_loop(low, high, one, 0)

    barrier = pltpu.get_barrier_semaphore()
    for d in range(1, n):
        pl.semaphore_signal(barrier, inc=1, device_id={axis: lax.rem(me + d, n)},
                            device_id_type=pl.DeviceIdType.MESH)

    fetch = [pltpu.make_async_copy(a, b, in_s.at[i]) for i, (a, b) in enumerate(
        ((kl_h, kl), (v_h, v), (ql_h, ql), (g_h, g), (kw_h, kw), (qw_h, qw)))]
    for f in fetch:
        f.start()
    nown[...] = jnp.zeros_like(nown)
    nbown[...] = jnp.zeros_like(nbown)
    dden[...] = jnp.zeros_like(dden)
    stat[...] = jnp.zeros_like(stat)
    ones8 = jnp.ones((8, tok), BF)
    ones = jnp.ones((128, 128), BF)
    ones2 = jnp.ones((2 * tok, 128), BF)
    never = jnp.full((tok, tok), -1e30, F32)
    none = jnp.zeros((tok, tok), F32)
    tri[...] = jnp.where(causal, 1.0, 0.0)
    bias[:, :tok] = jnp.where(causal, none, never)
    bias[:, tok:] = jnp.where(jnp.logical_and(cols > rows, me > 0), none, never)
    later[...] = jnp.where(jnp.logical_and(rows > cols, me < n - 1), none, never)
    dkt[...] = jnp.zeros_like(dkt)

    @pl.when(first)
    def _():
        kprev[...] = jnp.zeros_like(kprev)
        vprev[...] = jnp.zeros_like(vprev)
        f_in[...] = jnp.zeros_like(f_in)

    @pl.when(last)
    def _():
        qnext[...] = jnp.zeros_like(qnext)
        gnext[...] = jnp.zeros_like(gnext)
        stat_in[...] = jnp.zeros_like(stat_in)
        b_in[...] = jnp.zeros_like(b_in)

    fetch[0].wait()
    kt[...] = kl[...].astype(F32).T
    fetch[1].wait()

    def pair_features(x, query):
        return jnp.concatenate([features(x[:FD], query), features(x[FD:], query)], 0).astype(BF)

    def phase_a(p):
        feats = pair_features(kt[prow(p), :], False)
        kf[p] = feats
        nown[pl.ds(2 * p, 1), 0:NF] = dot(ones8, feats[:NF], 1, 1)[0:1]
        nown[pl.ds(2 * p + 1, 1), 0:NF] = dot(ones8, feats[NF:], 1, 1)[0:1]
        s_own[p] = pick(dot(feats, v[:, cut(p)], 1, 0))

    loop(0, pairs, phase_a)
    pl.semaphore_wait(barrier, n - 1)
    loop(me + 1, n, lambda j: n_copy(j).start())

    def send_front(p):
        @pl.when(jnp.logical_not(last))
        def _():
            halo(0, p).start()
            halo(1, p).start()

    def send_back(p):
        @pl.when(jnp.logical_not(first))
        def _():
            halo(2, p).start()
            halo(3, p).start()

    fetch[2].wait()
    qt[...] = ql[...].astype(F32).T

    def spread_q(p):
        x = (qt[prow(p), :] * 0.25).astype(BF)
        z = jnp.zeros((FD, tok), BF)
        return jnp.concatenate(
            [jnp.concatenate([x[:FD], z], 0), jnp.concatenate([z, x[FD:]], 0)], 1)

    def phase_b(p):
        send_front(p)
        qf[p] = pair_features(qt[prow(p), :], True)
        s = dot(spread_q(p), kt[prow(p), :].astype(BF), 0, 0)
        mask = jnp.concatenate([tri[...], tri[...]], 0)
        kk = mask * (1.0 + s + 0.5 * s * s)
        low = kk.astype(BF)
        kern[p] = low
        plus[p] = mask * (1.0 + s)
        ksum[p] = pick(dot(low, ones, 1, 0))

    loop(0, pairs, phase_b)

    def gathered(low, high, arrive, slots):
        def one(j, total):
            arrive(j).wait_recv()
            return total + slots[j]
        total = lax.fori_loop(low, high, one, jnp.zeros(nown.shape, F32))
        full = jnp.concatenate([total, jnp.zeros((128 - heads, nown.shape[1]), F32)], 0)
        return full.T[0:NF].astype(BF)

    ncol[...] = gathered(0, me, n_from, nall)
    fetch[3].wait()

    def phase_c(p):
        prior = []
        for hh in range(2):
            every = dot(qf[p, hh * NF : (hh + 1) * NF], ncol[...], 0, 0)
            prior.append(jnp.sum(jnp.where(lanes2 == 2 * p + hh, every, 0.0), 1, keepdims=True))
        r = 1.0 / (ksum[p] + jnp.where(lane < DH, prior[0], prior[1]))
        rden[p] = r
        low = (g[:, cut(p)].astype(F32) * r).astype(BF)
        dn[:, cut(p)] = low
        sb_own[p] = pick(dot(qf[p], low, 1, 0))

    loop(0, pairs, phase_c)
    fetch[4].wait()
    fetch[5].wait()

    def window(p):
        c = cut(p)
        k = jnp.concatenate([kw[:, c], kprev[:, c]], 0)
        vv = jnp.concatenate([v[:, c], vprev[:, c]], 0)
        qs, gs = both_halves(qw[:, c], 0.125), both_halves(g[:, c])
        hidden = bias[...]
        s = dot(qs, k, 1, 1) + jnp.concatenate([hidden, hidden], 0)
        m = jnp.max(s, 1, keepdims=True)
        e = jnp.exp(s - m)
        res = dot(e.astype(BF), jnp.concatenate([vv, ones2], 1), 1, 0)
        total = res[:, 128:]
        inv = 1.0 / total
        a = e * jnp.concatenate([inv, inv], 1)
        low = a.astype(BF)
        res = res[:, :128] * inv
        inner = dot((gs.astype(F32) * res).astype(BF), ones, 1, 0)
        ds = (a * (dot(gs, vv, 1, 1) - jnp.concatenate([inner, inner], 1))).astype(BF)
        win[:, c] = pick(res)
        gqw[:, c] = (pick(dot(ds, k, 1, 0)) * 0.125).astype(BF)
        dwk[:, c] = dot(ds[:, :tok], qs, 0, 0)
        dwv[:, c] = dot(low[:, :tok], gs, 0, 0)
        logsum = m + jnp.log(total)
        old = stat[...]
        for hh in range(2):
            part = slice(hh * tok, (hh + 1) * tok)
            old = jnp.where(lanes2 == 2 * p + hh, logsum[part], old)
            old = jnp.where(lanes2 == heads + 2 * p + hh, inner[part], old)
        stat[...] = old

    def f_step(p):
        @pl.when(jnp.logical_not(first))
        def _():
            f_copy(p).wait_recv()

        @pl.when(jnp.logical_not(last))
        def _():
            f_out[p] = (f_in[p].astype(F32) + s_own[p]).astype(BF)
            f_copy(p).start()

    def b_step(p):
        @pl.when(jnp.logical_not(last))
        def _():
            b_copy(p).wait_recv()

        @pl.when(jnp.logical_not(first))
        def _():
            b_out[p] = (b_in[p].astype(F32) + sb_own[p]).astype(BF)
            b_copy(p).start()

    def phase_d(p):
        c = cut(p)
        vv, r, pre = v[:, c], rden[p], f_in[p]
        num = dot(kern[p], vv, 1, 0)
        num = jnp.where(lane < DH, num[:tok] + dot(qf[p, :NF], pre, 0, 0),
                        num[tok:] + dot(qf[p, NF:], pre, 0, 0))
        out = num * r
        mixed[:, c] = (out + win[:, c]).astype(BF)
        prod = g[:, c].astype(F32) * out * r
        dd = dot(both_halves(-prod.astype(BF)), ones, 1, 0)
        one_head = [jnp.where(lanes2 == 2 * p + hh, dd[hh * tok : (hh + 1) * tok], 0.0) for hh in range(2)]
        dden[...] += one_head[0] + one_head[1]
        dm = both_halves(dn[:, c])
        ds = (dot(dm, vv, 1, 1) + dd) * plus[p]
        ds = ds.astype(BF)
        d_feat = dot(jnp.concatenate([pre, ncol[...]], 1),
                     jnp.concatenate([dm, jnp.concatenate(one_head, 0).astype(BF)], 1), 1, 1)
        x = qt[prow(p), :]
        dq = dot(kt[prow(p), :].astype(BF), ds, 1, 1) * 0.25
        dqt[prow(p), :] = jnp.concatenate(
            [dq[:FD, :tok] + pull(x[:FD], d_feat[:, :tok], True),
             dq[FD:, tok:] + pull(x[FD:], d_feat[:, tok:], True)], 0)
        dkt[prow(p), :] += dot(spread_q(p), ds, 1, 0)

    def key_side(p):
        c = cut(p)
        q, gg = qnext[:, c], gnext[:, c]
        q = q * jnp.asarray(0.125, BF)
        s = dot(both_halves(kw[:, c]), q, 1, 1)
        da = dot(both_halves(v[:, c]), gg, 1, 1)
        aa, dd = [], []
        for hh in range(2):
            part = slice(hh * tok, (hh + 1) * tok)
            h = 2 * p + hh
            a = jnp.exp(s[part] - stat_in[pl.ds(h, 1), :] + later[...])
            aa.append(a.astype(BF))
            dd.append((a * (da[part] - stat_in[pl.ds(heads + h, 1), :])).astype(BF))
        dk = dot(jnp.concatenate(dd, 1), both_halves(q), 1, 0)
        gkw[:, c] = (dwk[:, c] + dk).astype(BF)
        dwv[:, c] += dot(jnp.concatenate(aa, 1), both_halves(gg), 1, 0)

    def phase_e(p):
        c = cut(p)
        vv, post = v[:, c], b_in[p]
        dv = dot(kern[p], both_halves(dn[:, c]), 0, 0) + dot(kf[p], both_halves(post), 0, 0)
        dwv[:, c] += dv
        pull_keys(p, dot(post, both_halves(vv), 1, 1))

    def pull_keys(p, d_feat):
        x = kt[prow(p), :]
        dkt[prow(p), :] += jnp.concatenate(
            [pull(x[:FD], d_feat[:, :tok], False), pull(x[FD:], d_feat[:, tok:], False)], 0)

    def back_norm(h):
        one = jnp.broadcast_to(dden[pl.ds(h, 1), :], (8, tok)).astype(BF)
        feats = qf[h // 2, pl.ds(pl.multiple_of(lax.rem(h, 2) * NF, 16), NF), :]
        nbown[pl.ds(h, 1), 0:NF] = dot(one, feats, 1, 1)[0:1]

    def finish(p):
        c = cut(p)
        gv[:, c] = dwv[:, c].astype(BF)
        one_head = [jnp.where(lanes2 == 2 * p + hh, 1.0, 0.0).astype(BF) for hh in range(2)]
        pull_keys(p, dot(nbcol[...], jnp.concatenate(one_head, 0), 1, 1))

    hop = 2
    turns = max(hop * (n - 1), pairs) + pairs
    key_at = max(pairs + 2, turns - 6)
    d_at = jnp.maximum(pairs, hop * me)
    e_at = jnp.maximum(pairs, hop * (n - 1 - me))

    def within(p, body):
        @pl.when(jnp.logical_and(p >= 0, p < pairs))
        def _():
            body(p)

    def front_here(p):
        halo(0, p).wait_recv()
        halo(1, p).wait_recv()

    def back_here(p):
        halo(2, p).wait_recv()
        halo(3, p).wait_recv()

    def wave(j):
        within(j - hop * me, f_step)
        within(j - hop * (n - 1 - me), b_step)

        @pl.when(jnp.logical_and(j == 0, jnp.logical_not(first)))
        def _():
            loop(0, pairs, front_here)

        @pl.when(j < pairs)
        def _():
            window(j)

        @pl.when(j == pairs - 1)
        def _():
            stat_t[...] = stat[...].T[0 : 2 * heads]

            @pl.when(jnp.logical_not(first))
            def _():
                stats_copy().start()

        within(j - 4, send_back)
        within(j - d_at, phase_d)

        @pl.when(j == d_at + pairs - 1)
        def _():
            dden[...] = dden[...].T
            loop(0, heads, back_norm)
            loop(0, me, lambda i: nb_copy(i).start())

        within(j - e_at, phase_e)

        @pl.when(jnp.logical_and(j == key_at, jnp.logical_not(last)))
        def _():
            loop(0, pairs, back_here)
            stats_copy().wait_recv()

        within(j - key_at, key_side)

    loop(0, turns, wave)
    loop(min(turns - key_at, pairs), pairs, key_side)
    gql[...] = dqt[...].T.astype(BF)
    nbcol[...] = gathered(me + 1, n, nb_from, nball)
    loop(0, pairs, finish)
    gkl[...] = dkt[...].T.astype(BF)

    def drain(p):
        @pl.when(jnp.logical_not(last))
        def _():
            halo(0, p).wait_send()
            halo(1, p).wait_send()
            f_copy(p).wait_send()

        @pl.when(jnp.logical_not(first))
        def _():
            halo(2, p).wait_send()
            halo(3, p).wait_send()
            b_copy(p).wait_send()

    loop(0, pairs, drain)
    loop(me + 1, n, lambda j: n_copy(j).wait_send())
    loop(0, me, lambda j: nb_copy(j).wait_send())

    @pl.when(jnp.logical_not(first))
    def _():
        stats_copy().wait_send()


def writer(*refs):
    count = 6
    held, load_s, store_s = refs[2 * count : 3 * count], refs[-2], refs[-1]
    loads = [pltpu.make_async_copy(refs[i], held[i], load_s.at[i]) for i in range(count)]
    stores = [pltpu.make_async_copy(held[i], refs[count + i], store_s.at[i]) for i in range(count)]
    for c in loads:
        c.start()
    for c, d in zip(loads, stores):
        c.wait()
        d.start()
    for d in stores:
        d.wait()


def local(n, axis, *args):
    ql, v = args[0], args[4]
    tok, width = v.shape
    lin = ql.shape[1]
    pairs = width // 128
    heads = 2 * pairs
    vm = pltpu.VMEM
    dma = pltpu.SemaphoreType.DMA
    state16 = vm((pairs, NF, 128), BF)
    state32 = vm((pairs, NF, 128), F32)
    rows = vm((heads, 256), F32)
    wide32 = vm((tok, width), F32)
    wide16 = vm((tok, width), BF)
    lin16 = vm((tok, lin), BF)
    lin32 = vm((lin, tok), F32)
    tile32 = vm((pairs, tok, 128), F32)
    feats = vm((pairs, 2 * NF, tok), BF)
    small = vm((tok, 128), F32)
    scratch = [
        lin16, lin16, wide16, wide16, wide16, wide16,
        vm((tok, 2 * tok), F32), vm((tok, tok), F32), vm((tok, tok), F32),
        lin32, lin32, feats, feats, vm((pairs, 2 * tok, tok), BF), vm((pairs, 2 * tok, tok), F32), tile32,
        rows, vm((n, heads, 256), F32), vm((NF, 128), BF), state32, state16, state16,
        state32, state16, state16, tile32, wide16, wide32, wide32, wide32,
        small, small, vm((2 * heads, tok), F32), vm((2 * heads, tok), F32),
        rows, vm((n, heads, 256), F32), vm((NF, 128), BF),
        wide16, wide16, wide16, wide16, lin32, lin32,
        dma((6,)), dma((4, pairs)), dma((4, pairs)), dma((n,)), dma((n,)), dma((n,)), dma((n,)),
        dma((pairs,)), dma((pairs,)), dma((pairs,)), dma((pairs,)), dma, dma,
    ]
    order = (v, ql, ql, v, v, v)
    shapes = tuple(jax.ShapeDtypeStruct(a.shape, BF) for a in order)
    hbm = pl.BlockSpec(memory_space=pltpu.HBM)
    anywhere = pl.BlockSpec(memory_space=pl.ANY)
    made = pl.pallas_call(
        functools.partial(kernel, n, axis),
        out_shape=shapes,
        in_specs=[hbm] * 6,
        out_specs=tuple([pl.BlockSpec(memory_space=pltpu.VMEM)] * 6),
        scratch_shapes=scratch,
        compiler_params=pltpu.CompilerParams(
            collective_id=0, has_side_effects=True, vmem_limit_bytes=60 * 1024 * 1024),
    )(*args)
    return pl.pallas_call(
        writer,
        out_shape=shapes,
        in_specs=[anywhere] * 6,
        out_specs=tuple([anywhere] * 6),
        scratch_shapes=[vm(a.shape, BF) for a in order] + [dma((6,)), dma((6,))],
        compiler_params=pltpu.CompilerParams(vmem_limit_bytes=60 * 1024 * 1024),
    )(*made)


def solution(mesh):
    place = P(("dp", "seq"), None)
    return jax.shard_map(
        functools.partial(local, mesh.shape["seq"], "seq"),
        mesh=mesh,
        in_specs=(place,) * 6,
        out_specs=(place,) * 6,
        check_vma=False,
    )
```
